256 devices in a mesh: pipe: 4 (over z_lo, core), expert: 64 (over z_hi, x, y).
Axes of the slice: x: 4, y: 4, z: 8 (z_hi: 4, z_lo: 2; z = z_hi * 2 + z_lo), core: 2. Of those that a mesh axis runs over, the one named last changes fastest.
Arguments:
- out_grad: bfloat16 [4, 2, 4096, 7168], P('pipe', None, 'expert'), may hold values from -6 to 6
- expert_ids: int32 [4, 2, 4096, 1], P('pipe', None, 'expert'), may hold values from 0 to 7; in each aligned block of 64 rows (0 to 63, 64 to 127, ..., all dimensions but the last counted through in order) at most 9 rows name the same one
- gate_weights: float32 [4, 2, 4096, 1], P('pipe', None, 'expert'), may hold values from 0.1 to 1
- valid: int32 [4, 2, 4096], P('pipe', None, 'expert'), may hold values 0 or 1
- gate_pre: bfloat16 [4, 2, 576, 8192], P('pipe', None, None, 'expert'), may hold values from -8 to 8
- up_pre: bfloat16 [4, 2, 576, 8192], P('pipe', None, None, 'expert'), may hold values from -6 to 6
- w_gate: bfloat16 [4, 57344, 1024], P('pipe', 'expert'), may hold values from -0.1875 to 0.1875
- w_up: bfloat16 [4, 57344, 1024], P('pipe', 'expert'), may hold values from -0.1875 to 0.1875
- w_down: bfloat16 [4, 1024, 57344], P('pipe', None, 'expert'), may hold values from -0.0625 to 0.0625
Outputs:
- grad_in: bfloat16 [4, 2, 4096, 7168], P('pipe', None, 'expert')
The draws below stay inside these ranges and needn't reach their ends.
Inputs may be any that keep to these rules, and one draw needn't show every extreme that they name: `expert_ids`: A token's 1 ids differ. Among the 64 rows of one device for one section and micro-batch no expert is named more than 9 times, and in some such blocks one is named exactly 9 times.
All inputs are finite; a program needn't handle non-finite values. No bound on the sum of `valid` on one device may be relied on, other than what follows from the above.
Results may differ from the reference program's by a relative error of at most 0.0058.
Values may be sent and summed in bfloat16 or wider, within the bound.
A program may use at most 64 MiB of HBM per device.

```python
import math
import jax
import jax.numpy as jnp
import numpy as np
from jax import lax

D = 7168
HID = 1024
LAYER_EXPERTS = 8
TOPK = 1
MB = 2
TOK_DEV = 64
SECTIONS = 4
TOKENS = 4096
CAP = 9
N_EXPERT = 64


def plant(entries, rng, smallest, largest):
    index_at = [jax.random.randint(jax.random.fold_in(rng, axis), (), 0, length) for axis, length in enumerate(entries.shape)]
    widest = entries.shape.index(max(entries.shape))
    neighbour = index_at[:widest] + [(index_at[widest] + 1) % entries.shape[widest]] + index_at[widest + 1:]
    return entries.at[tuple(index_at)].set(smallest).at[tuple(neighbour)].set(largest)


def level_of(own_key, dims, shards, smallest, high):
    level, own = 1.0, jax.random.fold_in(own_key, 6)
    for axis_at, parts in shards:
        steps = jnp.exp(jax.random.uniform(jax.random.fold_in(own, axis_at), (parts,), jnp.float32, smallest / len(shards), high / len(shards)))
        level = level * jnp.repeat(steps, dims[axis_at] // parts).reshape([-1 if axis == axis_at else 1 for axis in range(len(dims))])
    return level


def deal_out(rng, own, number, rows, amount, top, limit, slope):
    ranking = jax.random.permutation(rng, amount)
    crowded, usual = load_shares(amount, rows * top, limit, slope, True), load_shares(amount, rows * top, limit, slope, False)
    places = jnp.arange(amount)

    def named(lengths, rotation):
        used = int((lengths > 0).sum())
        fixed = max(1, used // 4)
        shifted = fixed + (places - fixed + rotation * (used - fixed)) % max(1, amount - fixed)
        return jnp.zeros((amount,), jnp.int32).at[ranking[jnp.where(places < fixed, places, shifted)]].set(jnp.asarray(lengths, jnp.int32))

    lengths = jnp.where(number % 4 == 0, named(crowded, number // 4), named(usual, number - number // 4 - 1))
    mixed = jax.random.permutation(jax.random.fold_in(own, 3), amount)
    donor, taker = mixed[0:amount // 2 * 2:2], mixed[1:amount // 2 * 2:2]
    slack = jnp.minimum(lengths[donor] - 1, limit - lengths[taker]) // 2
    slack = jnp.where((donor == ranking[0]) | (taker == ranking[0]) | (lengths[taker] == 0), 0, jnp.maximum(slack, 0))
    shifted = jax.random.randint(jax.random.fold_in(own, 4), (amount // 2,), 0, 1 << 20) % (slack + 1)
    lengths = lengths.at[donor].add(-shifted).at[taker].add(shifted)
    members = jnp.searchsorted(jnp.cumsum(lengths), jnp.arange(rows * top), side="right").astype(jnp.int32)
    listing = members.reshape(top, rows).T
    listing = listing[jax.random.permutation(jax.random.fold_in(own, 1), rows)]
    rotation = jax.random.randint(jax.random.fold_in(own, 2), (rows, 1), 0, top)
    return jnp.take_along_axis(listing, (jnp.arange(top)[None, :] + rotation) % top, axis=1)


def load_shares(number_of, total, bound, lean, full):
    portions = [(1 << 20) // math.isqrt(rank ** lean) + 1 for rank in range(1, number_of + 1)]
    largest = bound if full else min(bound, max(-(-total // number_of), total * portions[0] // sum(portions)))
    least = 1 if total - largest >= number_of - 1 else 0
    holding, surplus = [largest] + [least] * (number_of - 1), total - largest - least * (number_of - 1)
    while surplus > 0:
        movable = [i for i in range(1, number_of) if holding[i] < largest] or [i for i in range(1, number_of) if holding[i] < bound]
        pool, remaining = sum([portions[i] for i in movable]), surplus
        for i in movable:
            more = min(bound - holding[i], max(1, remaining * portions[i] // pool), surplus)
            holding[i] = holding[i] + more
            surplus = surplus - more
    return np.array(holding)


def bell_draw(rng, dims, deviation, most, cuts=(), kind=jnp.bfloat16):
    values = jax.random.normal(rng, dims, jnp.float32) * deviation
    if len(cuts) > 0:
        values = level_of(rng, dims, cuts, -0.22, 0.18) * values
    return jnp.clip(values, min=-most, max=most).astype(kind)


def setup_inputs(seed: int = 0) -> dict:
    splits = jax.random.split(jax.random.key(seed), 10)
    out_grad = bell_draw(splits[0], (SECTIONS, MB, TOKENS, D), 1.0, 6.0, ((0, 4), (2, 64)))
    expert_ids_keys = jax.random.split(jax.random.fold_in(splits[1], 1), SECTIONS * MB * TOKENS // TOK_DEV)
    expert_ids_turns = jax.random.permutation(jax.random.fold_in(splits[1], 3), SECTIONS * MB * TOKENS // TOK_DEV)
    expert_ids = jax.vmap(lambda own, number: deal_out(jax.random.fold_in(splits[1], 2), own, number, TOK_DEV, LAYER_EXPERTS, TOPK, CAP, 1))(expert_ids_keys, expert_ids_turns).reshape((SECTIONS, MB, TOKENS, TOPK))
    gate_weights = jnp.clip(jnp.exp(math.log(1.0) - 2.3025851 * jax.random.uniform(splits[2], (SECTIONS, MB, TOKENS, TOPK), jnp.float32) ** level_of(splits[2], (SECTIONS, MB, TOKENS, TOPK), ((0, 4), (2, 64)), -0.2, 0.2)), 0.1, 1.0)
    valid = plant((jax.random.randint(splits[3], (SECTIONS, MB, TOKENS), 0, 8) < 7).astype(jnp.int32), jax.random.fold_in(splits[3], 1), 0, 1)
    gate_pre = bell_draw(splits[4], (SECTIONS, MB, N_EXPERT * CAP, LAYER_EXPERTS * HID), 1.5, 8.0, ((0, 4), (3, 64)))
    up_pre = bell_draw(splits[5], (SECTIONS, MB, N_EXPERT * CAP, LAYER_EXPERTS * HID), 1.0, 6.0, ((0, 4), (3, 64)))
    w_gate = bell_draw(splits[6], (SECTIONS, LAYER_EXPERTS * D, HID), HID ** -0.5, 0.1875, ((0, 4), (1, 64)))
    w_up = bell_draw(splits[7], (SECTIONS, LAYER_EXPERTS * D, HID), HID ** -0.5, 0.1875, ((0, 4), (1, 64)))
    w_down = bell_draw(splits[8], (SECTIONS, HID, LAYER_EXPERTS * D), D ** -0.5, 0.0625, ((0, 4), (2, 64)))
    return dict(out_grad=out_grad, expert_ids=expert_ids, gate_weights=gate_weights, valid=valid, gate_pre=gate_pre, up_pre=up_pre, w_gate=w_gate, w_up=w_up, w_down=w_down)


def routed_grad(grad_out, route_ids, route_gates, valid_rows, gate_saved, up_saved, gate_weight_matrix, up_weight_matrix, down_weight_matrix):
    pair_ids = route_ids.reshape(N_EXPERT, TOK_DEV * TOPK).astype(jnp.int32)
    onehot = (pair_ids[..., None] == jnp.arange(LAYER_EXPERTS, dtype=jnp.int32)).astype(jnp.int32)
    before = jnp.cumsum(onehot, axis=1) - onehot
    slot_ids = lax.optimization_barrier(jnp.sum(before * onehot, axis=-1)).astype(jnp.int32)
    source_ids = jnp.broadcast_to(jnp.arange(N_EXPERT, dtype=jnp.int32)[:, None], pair_ids.shape)
    pair_scale = route_gates * valid_rows[:, None].astype(jnp.float32)
    pair_rows = (grad_out.astype(jnp.float32)[:, None, :] * pair_scale[..., None]).astype(jnp.bfloat16)
    pair_rows = pair_rows.reshape(N_EXPERT, TOK_DEV * TOPK, D)
    routed = jnp.zeros((LAYER_EXPERTS, N_EXPERT, CAP, D), jnp.bfloat16).at[pair_ids, source_ids, slot_ids].set(pair_rows)
    row_count = N_EXPERT * CAP
    routed = routed.reshape(LAYER_EXPERTS, row_count, D).astype(jnp.float32)
    down_rows = down_weight_matrix.reshape(HID, LAYER_EXPERTS, D).transpose(1, 0, 2).astype(jnp.float32)
    hidden_grad = jnp.einsum('erd,ehd->erh', routed, down_rows)
    gate_val = gate_saved.reshape(row_count, LAYER_EXPERTS, HID).transpose(1, 0, 2).astype(jnp.float32)
    up_val = up_saved.reshape(row_count, LAYER_EXPERTS, HID).transpose(1, 0, 2).astype(jnp.float32)
    sigmoid_g = jax.nn.sigmoid(gate_val)
    gate_grad = (hidden_grad * up_val * sigmoid_g * (1.0 + gate_val * (1.0 - sigmoid_g))).astype(jnp.bfloat16)
    up_grad = (hidden_grad * gate_val * sigmoid_g).astype(jnp.bfloat16)
    gate_rows = gate_weight_matrix.reshape(LAYER_EXPERTS, D, HID).astype(jnp.float32)
    up_rows = up_weight_matrix.reshape(LAYER_EXPERTS, D, HID).astype(jnp.float32)
    row_grads = jnp.einsum('erh,edh->erd', gate_grad.astype(jnp.float32), gate_rows)
    row_grads = row_grads + jnp.einsum('erh,edh->erd', up_grad.astype(jnp.float32), up_rows)
    row_grads = row_grads.astype(jnp.bfloat16).reshape(LAYER_EXPERTS, N_EXPERT, CAP, D)
    selected_rows = row_grads[pair_ids, source_ids, slot_ids].astype(jnp.float32)
    return lax.optimization_barrier(jnp.sum(selected_rows.reshape(TOKENS, TOPK, D), axis=1)).astype(jnp.bfloat16)

def reference(out_grad, expert_ids, gate_weights, valid, gate_pre, up_pre, w_gate, w_up, w_down):
    results = []
    for section_pos in range(SECTIONS):
        per_micro = []
        for micro_pos in range(MB):
            per_micro.append(routed_grad(out_grad[section_pos, micro_pos], expert_ids[section_pos, micro_pos], gate_weights[section_pos, micro_pos], valid[section_pos, micro_pos], gate_pre[section_pos, micro_pos], up_pre[section_pos, micro_pos], w_gate[section_pos], w_up[section_pos], w_down[section_pos]))
        results.append(per_micro)
    empty = jnp.zeros((TOKENS, D), jnp.bfloat16)
    sections_out = []
    for section_pos in range(SECTIONS):
        first = results[section_pos + 1][0] if section_pos + 1 < SECTIONS else empty
        second = results[section_pos - 1][1] if section_pos > 0 else empty
        sections_out.append(jnp.stack([first, second], axis=0))
    return jnp.stack(sections_out, axis=0)
```

```python
import jax
import jax.numpy as jnp
from jax import lax
from jax.experimental import pallas as pl
from jax.experimental.pallas import tpu as pltpu
from jax.sharding import PartitionSpec as P

EXPERTS = 8
MEMBERS = 8
CAP = 9
TOK = 64
LANES = 128
CHUNKS = 7
SLICE = CHUNKS * LANES
BLOCK = 64
SOURCES = 16
GROUP_ROWS = SOURCES * CAP
STACK = CHUNKS * GROUP_ROWS
ROWS = 4 * GROUP_ROWS
MESH = pl.DeviceIdType.MESH
F32 = jnp.float32
BF16 = jnp.bfloat16


def dot(a, b):
    return jnp.dot(a, b, preferred_element_type=F32)


def dot_t(a, b):
    return lax.dot_general(a, b, (((1,), (1,)), ((), ())), preferred_element_type=F32)


def iota(shape, axis):
    return lax.broadcasted_iota(jnp.int32, shape, axis)


def as_one(mask):
    return jnp.where(mask, 1.0, 0.0).astype(BF16)


def loop(count, step):
    def run(i, carry):
        step(i)
        return carry

    lax.fori_loop(0, count, run, 0)


def selection(ids):
    wide = 8 * TOK
    named = jnp.where(ids == iota((EXPERTS, wide), 0), 1.0, 0.0)
    row, col = iota((wide, wide), 0), iota((wide, wide), 1)
    ahead = as_one(((row >> 6) == (col >> 6)) & (row < col))
    before = dot(named.astype(BF16), ahead)
    slot = jnp.sum(named * before, axis=0, keepdims=True).astype(jnp.int32)
    chunk = iota((1, wide), 1) >> 6
    target = jnp.where(ids[0:1] >= 0, ids[0:1] * BLOCK + chunk * CAP + slot, -1)
    return jnp.where(row == target, 1.0, 0.0)


def kernel(
    ids_ref,
    scale_ref,
    x_ref,
    gate_ref,
    up_ref,
    wg_hbm,
    wu_hbm,
    wd_hbm,
    out_ref,
    wg_ref,
    wu_ref,
    wd_ref,
    sel_ref,
    back_ref,
    ids_in,
    pack_ref,
    unpack_ref,
    send_ref,
    recv_ref,
    rows_ref,
    part_ref,
    parts_ref,
    grads_ref,
    ret_ref,
    home_ref,
    w_sem,
    ids_send,
    ids_recv,
    d_send,
    d_recv,
    d_local,
    s_send,
    s_recv,
    s_local,
    g_send,
    g_recv,
    r_send,
    r_recv,
):
    p = lax.axis_index("pipe")
    me = lax.axis_index("expert")
    pipes = lax.axis_size("pipe")
    count = lax.axis_size("expert")
    group, member = me // MEMBERS, lax.rem(me, MEMBERS)
    first = group * MEMBERS
    half, y = member // 4, lax.rem(member, 4)
    across = first + lax.rem(member + 4, MEMBERS)
    has_low, has_high = p > 0, p < pipes - 1
    low, high = jnp.maximum(p - 1, 0), jnp.minimum(p + 1, pipes - 1)

    weights = [
        pltpu.make_async_copy(wd_hbm, wd_ref, w_sem.at[0]),
        pltpu.make_async_copy(wg_hbm, wg_ref, w_sem.at[1]),
        pltpu.make_async_copy(wu_hbm, wu_ref, w_sem.at[2]),
    ]
    for copy in weights:
        copy.start()

    barrier = pltpu.get_barrier_semaphore()

    def greet(i):
        pl.semaphore_signal(
            barrier, inc=1, device_id=(p, lax.rem(me + 1 + i, count)), device_id_type=MESH
        )

    loop(count - 1, greet)

    @pl.when(has_low)
    def _():
        pl.semaphore_signal(barrier, inc=1, device_id=(low, me), device_id_type=MESH)

    @pl.when(has_high)
    def _():
        pl.semaphore_signal(barrier, inc=1, device_id=(high, me), device_id_type=MESH)

    sel_ref[0] = selection(ids_ref[0]).astype(BF16)
    sel_ref[1] = selection(ids_ref[1]).astype(BF16)

    pl.semaphore_wait(
        barrier, count - 1 + jnp.where(has_low, 1, 0) + jnp.where(has_high, 1, 0)
    )

    def remote(src, dst, send, recv, device):
        return pltpu.make_async_remote_copy(
            src_ref=src,
            dst_ref=dst,
            send_sem=send,
            recv_sem=recv,
            device_id=device,
            device_id_type=MESH,
        )

    def drain(ref, sem):
        pltpu.make_async_copy(ref, ref, sem).wait()

    to_low = remote(ids_ref.at[0], ids_in.at[0], ids_send.at[0], ids_recv.at[0], (low, me))
    to_high = remote(ids_ref.at[1], ids_in.at[1], ids_send.at[1], ids_recv.at[1], (high, me))

    @pl.when(has_low)
    def _():
        to_low.start()

    @pl.when(has_high)
    def _():
        to_high.start()

    def dispatch(m):
        def part(i):
            s = lax.rem(member + i, MEMBERS)
            col = pl.multiple_of(s * SLICE, LANES)
            x = x_ref[m, :, pl.ds(col, SLICE)].astype(F32) * scale_ref[m]
            x = x.astype(BF16)
            x = jnp.concatenate([x[:, LANES * j : LANES * (j + 1)] for j in range(CHUNKS)], axis=0)
            o = dot(sel_ref[m, :, 0 : CHUNKS * TOK], x).astype(BF16)
            for e in range(EXPERTS):
                send_ref[m, e * MEMBERS + s] = o[BLOCK * e : BLOCK * (e + 1)]

            def go(k):
                d = lax.rem(group + k, EXPERTS) * MEMBERS + s
                src, dst = send_ref.at[m, d], recv_ref.at[m, me]

                @pl.when(d != me)
                def _():
                    remote(src, dst, d_send.at[m], d_recv.at[m], (p, d)).start()

                @pl.when(d == me)
                def _():
                    pltpu.make_async_copy(src, dst, d_local.at[m]).start()

            loop(EXPERTS, go)

        loop(MEMBERS, part)

    def hidden(m):
        drain(recv_ref.at[m, pl.ds(0, count - 1)], d_recv.at[m])
        drain(recv_ref.at[m, 0], d_local.at[m])

        def gather(i):
            pair = [recv_ref[m, pl.ds((2 * i + k) * SOURCES, SOURCES)] for k in range(2)]
            pair = jnp.concatenate([b.reshape(SOURCES * BLOCK, LANES) for b in pair], axis=1)
            rows = dot(pack_ref[...], pair).astype(BF16)
            for k in range(2):
                at = pl.multiple_of((2 * i + k) * GROUP_ROWS, 16)
                for j in range(CHUNKS):
                    rows_ref[pl.ds(at, GROUP_ROWS), LANES * j : LANES * (j + 1)] = rows[
                        GROUP_ROWS * j : GROUP_ROWS * (j + 1), LANES * k : LANES * (k + 1)
                    ]

        loop(2, gather)

        def part(i):
            pair = lax.rem(member // 2 + i, 4)
            w = wd_ref[pl.ds(pl.multiple_of(pair * 256, 256), 256), :]
            h = dot_t(rows_ref[...], w).astype(BF16)
            for k in range(2):
                j = 2 * pair + k
                part_ref[m, j] = h[:, LANES * k : LANES * (k + 1)]
                src, dst = part_ref.at[m, j], parts_ref.at[m, member]

                @pl.when(j != member)
                def _():
                    remote(src, dst, s_send.at[m], s_recv.at[m], (p, first + j)).start()

                @pl.when(j == member)
                def _():
                    pltpu.make_async_copy(src, dst, s_local.at[m]).start()

        loop(4, part)

    def activation(m):
        drain(parts_ref.at[m, pl.ds(0, MEMBERS - 1)], s_recv.at[m])
        drain(parts_ref.at[m, 0], s_local.at[m])

        def part(i):
            at = pl.ds(pl.multiple_of(i * GROUP_ROWS, 16), GROUP_ROWS)
            h = parts_ref[m, 0, at, :].astype(F32)
            for k in range(1, MEMBERS):
                h = h + parts_ref[m, k, at, :].astype(F32)
            g = gate_ref[m, at, :].astype(F32)
            u = up_ref[m, at, :].astype(F32)
            sig = jax.nn.sigmoid(g)
            grads_ref[m, 0, member, at, :] = (h * u * sig * (1.0 + g * (1.0 - sig))).astype(BF16)
            grads_ref[m, 1, member, at, :] = (h * g * sig).astype(BF16)

        loop(4, part)

    def along_y(m, kind, which, slot):
        block = grads_ref.at[m, kind, which]
        for k in (2, 1, 3):
            d = first + half * 4 + lax.rem(y + k, 4)
            remote(block, block, g_send.at[m, slot], g_recv.at[m, slot], (p, d)).start()

    def over_x(m, kind, start, size, slot):
        block = grads_ref.at[m, kind, pl.ds(start, size)]
        remote(block, block, g_send.at[m, slot], g_recv.at[m, slot], (p, across)).start()

    def spread(m):
        over_x(m, 1, member, 1, 0)
        along_y(m, 0, member, 1)
        along_y(m, 1, member, 2)

    def pass_on(m):
        drain(grads_ref.at[m, 1, pl.ds(0, 1)], g_recv.at[m, 0])
        along_y(m, 1, lax.rem(member + 4, MEMBERS), 3)
        drain(grads_ref.at[m, 0, pl.ds(0, 3)], g_recv.at[m, 1])
        over_x(m, 0, half * 4, 4, 4)

    def spread_end(m):
        drain(grads_ref.at[m, 1, pl.ds(0, 3)], g_recv.at[m, 2])
        drain(grads_ref.at[m, 1, pl.ds(0, 3)], g_recv.at[m, 3])
        drain(grads_ref.at[m, 0, pl.ds(0, 4)], g_recv.at[m, 4])

    def rows_out(m, wanted, target):
        def part(i):
            zone = lax.rem(group // 2 + 2 + i, 4)
            at = pl.ds(pl.multiple_of(zone * GROUP_ROWS, 16), GROUP_ROWS)
            gate = jnp.concatenate([grads_ref[m, 0, k, at, :] for k in range(MEMBERS)], axis=1)
            up = jnp.concatenate([grads_ref[m, 1, k, at, :] for k in range(MEMBERS)], axis=1)
            r = (dot_t(gate, wg_ref[...]) + dot_t(up, wu_ref[...])).astype(BF16)
            r = jnp.concatenate([r[:, LANES * j : LANES * (j + 1)] for j in range(CHUNKS)], axis=0)
            r = dot(unpack_ref[...], r).astype(BF16)
            ret_ref[m, pl.ds(zone * SOURCES, SOURCES)] = r.reshape(SOURCES, BLOCK, LANES)

            @pl.when(wanted)
            def _():
                def go(k):
                    q = zone * SOURCES + lax.rem(me + k, SOURCES)
                    remote(
                        ret_ref.at[m, q], home_ref.at[m, me], r_send.at[m], r_recv.at[m], (target, q)
                    ).start()

                loop(SOURCES, go)

        loop(4, part)

    def finish(m, wanted):
        @pl.when(wanted)
        def _():
            drain(home_ref.at[m], r_recv.at[m])

            def part(s):
                blocks = [home_ref[m, e * MEMBERS + s] for e in range(EXPERTS)]
                o = dot(back_ref[m, 0 : CHUNKS * TOK], jnp.concatenate(blocks, axis=0)).astype(BF16)
                for j in range(CHUNKS):
                    col = pl.multiple_of(s * SLICE + LANES * j, LANES)
                    out_ref[m, :, pl.ds(col, LANES)] = o[TOK * j : TOK * (j + 1)]

            loop(MEMBERS, part)

        @pl.when(jnp.logical_not(wanted))
        def _():
            out_ref[m] = jnp.zeros(out_ref.shape[1:], BF16)

    dispatch(0)
    dispatch(1)

    k = lax.rem(iota((1, SOURCES * BLOCK), 1), BLOCK)
    s = iota((1, SOURCES * BLOCK), 1) >> 6
    j = (k * 57) >> 9
    place = jnp.where(k < CHUNKS * CAP, j * GROUP_ROWS + s * CAP + k - j * CAP, -1)

    def build_pack(i):
        at = pl.multiple_of(i * GROUP_ROWS, 16)
        shape = (GROUP_ROWS, SOURCES * BLOCK)
        pack_ref[pl.ds(at, GROUP_ROWS), :] = as_one(iota(shape, 0) + at == place)

    loop(CHUNKS, build_pack)
    r = iota((1, STACK), 1)
    j = jnp.zeros_like(r)
    for i in range(1, CHUNKS):
        j = j + jnp.where(r >= i * GROUP_ROWS, 1, 0)
    r = r - j * GROUP_ROWS
    s = (r * 57) >> 9
    origin = s * BLOCK + j * CAP + r - s * CAP

    def build_unpack(i):
        at = pl.multiple_of(i * 128, 128)
        unpack_ref[pl.ds(at, 128), :] = as_one(iota((128, STACK), 0) + at == origin)

    loop(SOURCES * BLOCK // 128, build_unpack)

    @pl.when(has_high)
    def _():
        drain(ids_in.at[0], ids_recv.at[0])
        back_ref[0] = selection(ids_in[0]).T.astype(BF16)

    @pl.when(has_low)
    def _():
        drain(ids_in.at[1], ids_recv.at[1])
        back_ref[1] = selection(ids_in[1]).T.astype(BF16)

    weights[0].wait()
    hidden(0)
    activation(0)
    spread(0)
    pass_on(0)
    hidden(1)
    weights[1].wait()
    weights[2].wait()
    spread_end(0)
    rows_out(0, has_low, low)
    activation(1)
    spread(1)
    pass_on(1)
    spread_end(1)
    rows_out(1, has_high, high)
    finish(0, has_high)
    finish(1, has_low)

    @pl.when(has_low)
    def _():
        drain(ids_in.at[0], ids_send.at[0])
        drain(home_ref.at[0], r_send.at[0])

    @pl.when(has_high)
    def _():
        drain(ids_in.at[1], ids_send.at[1])
        drain(home_ref.at[1], r_send.at[1])

    for m in range(2):
        drain(recv_ref.at[m, pl.ds(0, count - 1)], d_send.at[m])
        drain(parts_ref.at[m, pl.ds(0, MEMBERS - 1)], s_send.at[m])
        for slot, size in enumerate((1, 3, 3, 3, 4)):
            drain(grads_ref.at[m, 0, pl.ds(0, size)], g_send.at[m, slot])


def body(out_grad, expert_ids, gate_weights, valid, gate_pre, up_pre, w_gate, w_up, w_down):
    count = lax.axis_size("expert")
    ids = expert_ids[0, :, :, 0]
    ids = jnp.concatenate([jnp.tile(ids, (1, CHUNKS)), jnp.full_like(ids, -1)], axis=1)
    ids = jnp.broadcast_to(ids[:, None, :], (2, EXPERTS, 8 * TOK))
    scale = gate_weights[0] * valid[0][..., None].astype(F32)
    vmem = pl.BlockSpec(memory_space=pltpu.VMEM)
    hbm = pl.BlockSpec(memory_space=pl.ANY)
    dma = pltpu.SemaphoreType.DMA
    out = pl.pallas_call(
        kernel,
        out_shape=jax.ShapeDtypeStruct(out_grad.shape[1:], BF16),
        in_specs=[vmem] * 5 + [hbm] * 3,
        out_specs=vmem,
        scratch_shapes=[
            pltpu.VMEM(w_gate.shape[1:], BF16),
            pltpu.VMEM(w_up.shape[1:], BF16),
            pltpu.VMEM(w_down.shape[1:], BF16),
            pltpu.VMEM((2, EXPERTS * BLOCK, 8 * TOK), BF16),
            pltpu.VMEM((2, 8 * TOK, EXPERTS * BLOCK), BF16),
            pltpu.VMEM((2, EXPERTS, 8 * TOK), jnp.int32),
            pltpu.VMEM((STACK, SOURCES * BLOCK), BF16),
            pltpu.VMEM((SOURCES * BLOCK, STACK), BF16),
            pltpu.VMEM((2, count, BLOCK, LANES), BF16),
            pltpu.VMEM((2, count, BLOCK, LANES), BF16),
            pltpu.VMEM((ROWS, SLICE), BF16),
            pltpu.VMEM((2, MEMBERS, ROWS, LANES), BF16),
            pltpu.VMEM((2, MEMBERS, ROWS, LANES), BF16),
            pltpu.VMEM((2, 2, MEMBERS, ROWS, LANES), BF16),
            pltpu.VMEM((2, count, BLOCK, LANES), BF16),
            pltpu.VMEM((2, count, BLOCK, LANES), BF16),
            dma((3,)),
            dma((2,)),
            dma((2,)),
            dma((2,)),
            dma((2,)),
            dma((2,)),
            dma((2,)),
            dma((2,)),
            dma((2,)),
            dma((2, 5)),
            dma((2, 5)),
            dma((2,)),
            dma((2,)),
        ],
        compiler_params=pltpu.CompilerParams(
            collective_id=0, has_side_effects=True, vmem_limit_bytes=58 * 2**20
        ),
    )(ids, scale, out_grad[0], gate_pre[0], up_pre[0], w_gate[0], w_up[0], w_down[0])
    return out[None]


def solution(mesh):
    placed = (
        P("pipe", None, "expert", None),
        P("pipe", None, "expert", None),
        P("pipe", None, "expert", None),
        P("pipe", None, "expert"),
        P("pipe", None, None, "expert"),
        P("pipe", None, None, "expert"),
        P("pipe", "expert", None),
        P("pipe", "expert", None),
        P("pipe", None, "expert"),
    )
    return jax.shard_map(
        body, mesh=mesh, in_specs=placed, out_specs=P("pipe", None, "expert", None), check_vma=False
    )
```

```python
import jax
import jax.numpy as jnp
from jax import lax
from jax.experimental import pallas as pl
from jax.experimental.pallas import tpu as pltpu
from jax.sharding import PartitionSpec as P

EXPERTS = 8
MEMBERS = 8
CAP = 9
TOK = 64
LANES = 128
CHUNKS = 7
SLICE = CHUNKS * LANES
BLOCK = 64
SOURCES = 16
GROUP_ROWS = SOURCES * CAP
STACK = CHUNKS * GROUP_ROWS
ZONES = 4
GATE = (0, 3)
UP = (1, 2)
MESH = pl.DeviceIdType.MESH
F32 = jnp.float32
BF16 = jnp.bfloat16


def dot(a, b):
    return jnp.dot(a, b, preferred_element_type=F32)


def dot_t(a, b):
    return lax.dot_general(a, b, (((1,), (1,)), ((), ())), preferred_element_type=F32)


def iota(shape, axis):
    return lax.broadcasted_iota(jnp.int32, shape, axis)


def as_one(mask):
    return jnp.where(mask, 1.0, 0.0).astype(BF16)


def loop(count, step):
    def run(i, carry):
        step(i)
        return carry

    lax.fori_loop(0, count, run, 0)


def selection(ids):
    wide = 8 * TOK
    ahead = as_one(iota((TOK, TOK), 0) < iota((TOK, TOK), 1))
    named = jnp.where(ids == iota((EXPERTS, TOK), 0), 1.0, 0.0)
    slot = jnp.sum(named * dot(named.astype(BF16), ahead), axis=0, keepdims=True)
    line = iota((EXPERTS, TOK), 0)
    both = jnp.where(line == 0, ids.astype(F32), jnp.where(line == 1, slot, 0.0)).astype(BF16)
    col = iota((TOK, wide), 1)
    spread = dot(both, as_one((col & (TOK - 1)) == iota((TOK, wide), 0))).astype(jnp.int32)
    chunk = iota((1, wide), 1) >> 6
    target = spread[0:1] * BLOCK + chunk * CAP + spread[1:2]
    target = jnp.where(chunk < CHUNKS, target, -1)
    return jnp.where(iota((wide, wide), 0) == target, 1.0, 0.0)


def kernel(
    ids_ref,
    weight_ref,
    valid_ref,
    x_ref,
    gate_ref,
    up_ref,
    wg_hbm,
    wu_hbm,
    wd_hbm,
    out_ref,
    wg_ref,
    wu_ref,
    wd_ref,
    sel_ref,
    back_ref,
    ids_out,
    ids_in,
    pack_ref,
    unpack_ref,
    scaled_ref,
    send_ref,
    recv_ref,
    rows_ref,
    part_ref,
    xin_ref,
    own_ref,
    sum_ref,
    yin_ref,
    grads_ref,
    ret_ref,
    home_ref,
    w_sem,
    ids_send,
    ids_recv,
    d_send,
    d_recv,
    d_local,
    x_send,
    x_recv,
    s_send,
    s_recv,
    g_send,
    g_recv,
    r_send,
    r_recv,
):
    p = lax.axis_index("pipe")
    me = lax.axis_index("expert")
    pipes = lax.axis_size("pipe")
    count = lax.axis_size("expert")
    group, member = me // MEMBERS, lax.rem(me, MEMBERS)
    first = group * MEMBERS
    z, half, y = me // SOURCES, member // 4, lax.rem(member, 4)
    other, spot = lax.rem(member + 4, MEMBERS), lax.rem(me, SOURCES)
    right, left = half * 4 + lax.rem(y + 1, 4), half * 4 + lax.rem(y + 3, 4)
    has_low, has_high = p > 0, p < pipes - 1
    low, high = jnp.maximum(p - 1, 0), jnp.minimum(p + 1, pipes - 1)

    barrier = pltpu.get_barrier_semaphore()

    def greet(i):
        pl.semaphore_signal(
            barrier, inc=1, device_id=(p, lax.rem(me + 1 + i, count)), device_id_type=MESH
        )

    loop(count - 1, greet)

    @pl.when(has_low)
    def _():
        pl.semaphore_signal(barrier, inc=1, device_id=(low, me), device_id_type=MESH)

    @pl.when(has_high)
    def _():
        pl.semaphore_signal(barrier, inc=1, device_id=(high, me), device_id_type=MESH)

    weights = [
        pltpu.make_async_copy(wd_hbm, wd_ref, w_sem.at[0]),
        pltpu.make_async_copy(wg_hbm, wg_ref, w_sem.at[1]),
        pltpu.make_async_copy(wu_hbm, wu_ref, w_sem.at[2]),
    ]
    for copy in weights:
        copy.start()

    def remote(src, dst, send, recv, device):
        return pltpu.make_async_remote_copy(
            src_ref=src,
            dst_ref=dst,
            send_sem=send,
            recv_sem=recv,
            device_id=device,
            device_id_type=MESH,
        )

    def drain(ref, sem):
        pltpu.make_async_copy(ref, ref, sem).wait()

    def zone_of(k):
        return lax.rem(z + k, ZONES)

    for m in range(2):
        ids = ids_ref[m]
        sel_ref[m] = selection(ids).astype(BF16)
        ids_out[m] = jnp.broadcast_to(
            jnp.concatenate([ids, jnp.zeros_like(ids)], axis=1), (EXPERTS, LANES)
        )
        same = iota((TOK, TOK), 0) == iota((TOK, TOK), 1)
        scale = weight_ref[m] * valid_ref[m : m + 1].astype(F32)
        scale = jnp.sum(jnp.where(same, scale, 0.0), axis=1, keepdims=True)
        for j in range(CHUNKS):
            for s in range(MEMBERS):
                col = s * SLICE + j * LANES
                scaled_ref[m, s // 2, TOK * j : TOK * (j + 1), LANES * (s % 2) : LANES * (s % 2 + 1)] = (
                    x_ref[m, :, col : col + LANES].astype(F32) * scale
                ).astype(BF16)

    def form(dz):
        zone = zone_of(dz)

        def part(i):
            m, pair = i // 4, lax.rem(i, 4)
            rows = pl.ds(pl.multiple_of(zone * 2 * BLOCK, 2 * BLOCK), 2 * BLOCK)
            o = dot(sel_ref[m, rows, 0 : CHUNKS * TOK], scaled_ref[m, pair]).astype(BF16)
            for e in range(2):
                for k in range(2):
                    send_ref[zone * SOURCES + e * MEMBERS + 2 * pair + k, m] = o[
                        BLOCK * e : BLOCK * (e + 1), LANES * k : LANES * (k + 1)
                    ]

        loop(8, part)

    def dispatch(dz):
        zone, c = zone_of(dz), (ZONES - dz) % ZONES
        first_other = 1 if dz == 0 else 0

        def go(i):
            t = lax.rem(spot + first_other + i, SOURCES)
            d = zone * SOURCES + t
            remote(send_ref.at[d], recv_ref.at[c, spot], d_send.at[dz], d_recv.at[c], (p, d)).start()

        loop(SOURCES - first_other, go)
        if dz == 0:
            pltpu.make_async_copy(send_ref.at[me], recv_ref.at[0, spot], d_local).start()

    def hidden(c):
        if c == 0:
            drain(recv_ref.at[c, pl.ds(0, SOURCES - 1)], d_recv.at[c])
            drain(recv_ref.at[c, 0], d_local)
        else:
            drain(recv_ref.at[c], d_recv.at[c])
        both = [recv_ref[c, :, m].reshape(SOURCES * BLOCK, LANES) for m in range(2)]
        rows = dot(pack_ref[...], jnp.concatenate(both, axis=1)).astype(BF16)
        for m in range(2):
            for j in range(CHUNKS):
                rows_ref[GROUP_ROWS * m : GROUP_ROWS * (m + 1), LANES * j : LANES * (j + 1)] = rows[
                    GROUP_ROWS * j : GROUP_ROWS * (j + 1), LANES * m : LANES * (m + 1)
                ]

        def product(pair):
            w = wd_ref[pl.ds(pl.multiple_of(pair * 256, 256), 256), :]
            return dot_t(rows_ref[...], w)

        def give(i):
            o = product(2 * (1 - half) + i).astype(BF16)
            for k in range(2):
                part_ref[c, 2 * i + k] = o[:, LANES * k : LANES * (k + 1)]
            two = pl.ds(2 * i, 2)
            remote(
                part_ref.at[c, two], xin_ref.at[c, two], x_send.at[c], x_recv.at[c], (p, first + other)
            ).start()

        loop(2, give)

        def keep(i):
            o = product(2 * half + i)
            for k in range(2):
                own_ref[c, 2 * i + k] = o[:, LANES * k : LANES * (k + 1)]

        loop(2, keep)

    def reduce_x(c):
        drain(xin_ref.at[c], x_recv.at[c])

        def part(k):
            t = lax.rem(y + k, 4)
            o = own_ref[c, t] + xin_ref[c, t].astype(F32)

            @pl.when(k > 0)
            def _():
                sum_ref[c, t] = o.astype(BF16)
                remote(
                    sum_ref.at[c, t],
                    yin_ref.at[c, k - 1],
                    s_send.at[c],
                    s_recv.at[c],
                    (p, first + half * 4 + t),
                ).start()

            @pl.when(k == 0)
            def _():
                own_ref[c, t] = o

        loop(4, lambda i: part(lax.rem(i + 2, 4)))

    def activation(c):
        drain(yin_ref.at[c], s_recv.at[c])
        saved = pl.ds(pl.multiple_of(zone_of(c) * GROUP_ROWS, 16), GROUP_ROWS)
        for m in range(2):
            at = pl.ds(GROUP_ROWS * m, GROUP_ROWS)
            o = own_ref[c, y, at, :]
            for k in range(3):
                o = o + yin_ref[c, k, at, :].astype(F32)
            g = gate_ref[m, saved, :].astype(F32)
            u = up_ref[m, saved, :].astype(F32)
            sig = jax.nn.sigmoid(g)
            grads_ref[c, member, GATE[m]] = (o * u * sig * (1.0 + g * (1.0 - sig))).astype(BF16)
            grads_ref[c, member, UP[m]] = (o * g * sig).astype(BF16)
        share(c, 0, other, member, 0, 3)
        share(c, 1, right, member, 0, 4)
        share(c, 1, left, member, 0, 4)

    def share(c, slot, to, whose, start, size):
        block = grads_ref.at[c, whose, pl.ds(start, size)]
        remote(block, block, g_send.at[c, slot], g_recv.at[c, slot], (p, first + to)).start()

    def arrived(c, slot, quarters):
        drain(grads_ref.at[c, 0, pl.ds(0, quarters)], g_recv.at[c, slot])

    def pass_on(c):
        drain(grads_ref.at[c, 0, pl.ds(0, 3)], g_recv.at[c, 0])
        share(c, 2, right, other, 0, 3)
        share(c, 2, left, other, 0, 3)
        drain(grads_ref.at[c, pl.ds(0, 2)], g_recv.at[c, 1])
        share(c, 3, left, right, 0, 2)
        share(c, 3, right, left, 2, 2)

    def pass_far(c):
        drain(grads_ref.at[c, 0], g_recv.at[c, 3])
        block = grads_ref.at[c, pl.ds(half * 4, 4), 3]
        remote(block, block, g_send.at[c, 5], g_recv.at[c, 5], (p, first + other)).start()
        drain(grads_ref.at[c, pl.ds(0, 2), pl.ds(0, 3)], g_recv.at[c, 2])
        over_right = lax.rem(right + 4, MEMBERS)
        over_left = lax.rem(left + 4, MEMBERS)
        one, two = (left, right) if c % 2 == 0 else (right, left)
        over_one, over_two = (over_left, over_right) if c % 2 == 0 else (over_right, over_left)
        share(c, 4, one, over_two, 0, 2)
        share(c, 4, two, over_one, 2, 1)

    def rows_out(c):
        zone = zone_of(c)
        drain(grads_ref.at[c, 0, pl.ds(0, 3)], g_recv.at[c, 4])
        drain(grads_ref.at[c, pl.ds(0, 4), 0], g_recv.at[c, 5])

        def whole(quarters):
            rows = [
                jnp.concatenate([grads_ref[c, k, q] for k in range(MEMBERS)], axis=1)
                for q in quarters
            ]
            return jnp.concatenate(rows, axis=0)

        gate, up = whole(GATE), whole(UP)
        r = (dot_t(gate, wg_ref[...]) + dot_t(up, wu_ref[...])).astype(BF16)
        r = jnp.concatenate(
            [
                jnp.concatenate(
                    [
                        r[GROUP_ROWS * m : GROUP_ROWS * (m + 1), LANES * j : LANES * (j + 1)]
                        for m in range(2)
                    ],
                    axis=1,
                )
                for j in range(CHUNKS)
            ],
            axis=0,
        )
        r = dot(unpack_ref[...], r).astype(BF16)
        for m, wanted, target in ((0, has_low, low), (1, has_high, high)):
            ret_ref[m, pl.ds(zone * SOURCES, SOURCES)] = r[:, LANES * m : LANES * (m + 1)].reshape(
                SOURCES, BLOCK, LANES
            )

            @pl.when(wanted)
            def _():
                def go(k):
                    q = zone * SOURCES + lax.rem(me + k, SOURCES)
                    remote(
                        ret_ref.at[m, q], home_ref.at[m, me], r_send.at[m], r_recv.at[m], (target, q)
                    ).start()

                loop(SOURCES, go)

    def selections():
        @pl.when(has_high)
        def _():
            drain(ids_in.at[0], ids_recv.at[0])
            back_ref[0] = selection(ids_in[0, 0:1, 0:TOK]).T.astype(BF16)

        @pl.when(has_low)
        def _():
            drain(ids_in.at[1], ids_recv.at[1])
            back_ref[1] = selection(ids_in[1, 0:1, 0:TOK]).T.astype(BF16)

    def finish(m, wanted):
        @pl.when(wanted)
        def _():
            drain(home_ref.at[m], r_recv.at[m])

            def part(i):
                blocks = [
                    jnp.concatenate([home_ref[m, e * MEMBERS + 2 * i + k] for k in range(2)], axis=1)
                    for e in range(EXPERTS)
                ]
                o = dot(back_ref[m, 0 : CHUNKS * TOK], jnp.concatenate(blocks, axis=0)).astype(BF16)
                for k in range(2):
                    for j in range(CHUNKS):
                        col = pl.multiple_of((2 * i + k) * SLICE + LANES * j, LANES)
                        out_ref[m, :, pl.ds(col, LANES)] = o[
                            TOK * j : TOK * (j + 1), LANES * k : LANES * (k + 1)
                        ]

            loop(4, part)

        @pl.when(jnp.logical_not(wanted))
        def _():
            out_ref[m] = jnp.zeros(out_ref.shape[1:], BF16)

    def build_pack():
        k = lax.rem(iota((1, SOURCES * BLOCK), 1), BLOCK)
        s = iota((1, SOURCES * BLOCK), 1) >> 6
        j = (k * 57) >> 9
        place = jnp.where(k < CHUNKS * CAP, j * GROUP_ROWS + s * CAP + k - j * CAP, -1)

        def part(i):
            at = pl.multiple_of(i * GROUP_ROWS, 16)
            shape = (GROUP_ROWS, SOURCES * BLOCK)
            pack_ref[pl.ds(at, GROUP_ROWS), :] = as_one(iota(shape, 0) + at == place)

        loop(CHUNKS, part)

    def build_unpack():
        r = iota((1, STACK), 1)
        j = jnp.zeros_like(r)
        for i in range(1, CHUNKS):
            j = j + jnp.where(r >= i * GROUP_ROWS, 1, 0)
        r = r - j * GROUP_ROWS
        s = (r * 57) >> 9
        origin = s * BLOCK + j * CAP + r - s * CAP

        def part(i):
            at = pl.multiple_of(i * 128, 128)
            unpack_ref[pl.ds(at, 128), :] = as_one(iota((128, STACK), 0) + at == origin)

        loop(SOURCES * BLOCK // 128, part)

    form(2)
    pl.semaphore_wait(
        barrier, count - 1 + jnp.where(has_low, 1, 0) + jnp.where(has_high, 1, 0)
    )
    dispatch(2)
    form(0)
    dispatch(0)
    form(3)
    form(1)

    to_low = remote(ids_out.at[0], ids_in.at[0], ids_send.at[0], ids_recv.at[0], (low, me))
    to_high = remote(ids_out.at[1], ids_in.at[1], ids_send.at[1], ids_recv.at[1], (high, me))

    @pl.when(has_low)
    def _():
        to_low.start()

    @pl.when(has_high)
    def _():
        to_high.start()

    build_pack()
    weights[0].wait()
    hidden(0)
    reduce_x(0)
    dispatch(3)
    activation(0)
    hidden(2)
    pass_on(0)
    dispatch(1)
    hidden(1)
    reduce_x(2)
    activation(2)
    hidden(3)
    reduce_x(1)
    pass_on(2)
    pass_far(2)
    reduce_x(3)
    build_unpack()
    weights[1].wait()
    weights[2].wait()
    activation(1)
    rows_out(2)
    pass_on(1)
    pass_far(0)
    selections()
    activation(3)
    pass_far(1)
    pass_on(3)
    rows_out(1)
    pass_far(3)
    rows_out(3)
    rows_out(0)
    finish(0, has_high)
    finish(1, has_low)

    @pl.when(has_low)
    def _():
        drain(ids_in.at[0], ids_send.at[0])
        drain(home_ref.at[0], r_send.at[0])

    @pl.when(has_high)
    def _():
        drain(ids_in.at[1], ids_send.at[1])
        drain(home_ref.at[1], r_send.at[1])

    for c in range(ZONES):
        drain(recv_ref.at[c, pl.ds(0, SOURCES - (1 if c == 0 else 0))], d_send.at[c])
        drain(xin_ref.at[c], x_send.at[c])
        drain(yin_ref.at[c], s_send.at[c])
        drain(grads_ref.at[c, 0, pl.ds(0, 3)], g_send.at[c, 0])
        drain(grads_ref.at[c, pl.ds(0, 2)], g_send.at[c, 1])
        drain(grads_ref.at[c, pl.ds(0, 2), pl.ds(0, 3)], g_send.at[c, 2])
        drain(grads_ref.at[c, 0], g_send.at[c, 3])
        drain(grads_ref.at[c, 0, pl.ds(0, 3)], g_send.at[c, 4])
        drain(grads_ref.at[c, pl.ds(0, 4), 0], g_send.at[c, 5])


def body(out_grad, expert_ids, gate_weights, valid, gate_pre, up_pre, w_gate, w_up, w_down):
    count = lax.axis_size("expert")
    ids = expert_ids.reshape(2, 1, TOK)
    weight = gate_weights.reshape(2, 1, TOK)
    vmem = pl.BlockSpec(memory_space=pltpu.VMEM)
    hbm = pl.BlockSpec(memory_space=pl.ANY)
    dma = pltpu.SemaphoreType.DMA
    out = pl.pallas_call(
        kernel,
        out_shape=jax.ShapeDtypeStruct(out_grad.shape[1:], BF16),
        in_specs=[vmem] * 6 + [hbm] * 3,
        out_specs=vmem,
        scratch_shapes=[
            pltpu.VMEM(w_gate.shape[1:], BF16),
            pltpu.VMEM(w_up.shape[1:], BF16),
            pltpu.VMEM(w_down.shape[1:], BF16),
            pltpu.VMEM((2, EXPERTS * BLOCK, 8 * TOK), BF16),
            pltpu.VMEM((2, 8 * TOK, EXPERTS * BLOCK), BF16),
            pltpu.VMEM((2, EXPERTS, LANES), jnp.int32),
            pltpu.VMEM((2, EXPERTS, LANES), jnp.int32),
            pltpu.VMEM((STACK, SOURCES * BLOCK), BF16),
            pltpu.VMEM((SOURCES * BLOCK, STACK), BF16),
            pltpu.VMEM((2, 4, CHUNKS * TOK, 2 * LANES), BF16),
            pltpu.VMEM((count, 2, BLOCK, LANES), BF16),
            pltpu.VMEM((ZONES, SOURCES, 2, BLOCK, LANES), BF16),
            pltpu.VMEM((2 * GROUP_ROWS, SLICE), BF16),
            pltpu.VMEM((ZONES, 4, 2 * GROUP_ROWS, LANES), BF16),
            pltpu.VMEM((ZONES, 4, 2 * GROUP_ROWS, LANES), BF16),
            pltpu.VMEM((ZONES, 4, 2 * GROUP_ROWS, LANES), F32),
            pltpu.VMEM((ZONES, 4, 2 * GROUP_ROWS, LANES), BF16),
            pltpu.VMEM((ZONES, 3, 2 * GROUP_ROWS, LANES), BF16),
            pltpu.VMEM((ZONES, MEMBERS, 4, GROUP_ROWS, LANES), BF16),
            pltpu.VMEM((2, count, BLOCK, LANES), BF16),
            pltpu.VMEM((2, count, BLOCK, LANES), BF16),
            dma((3,)),
            dma((2,)),
            dma((2,)),
            dma((ZONES,)),
            dma((ZONES,)),
            dma,
            dma((ZONES,)),
            dma((ZONES,)),
            dma((ZONES,)),
            dma((ZONES,)),
            dma((ZONES, 6)),
            dma((ZONES, 6)),
            dma((2,)),
            dma((2,)),
        ],
        compiler_params=pltpu.CompilerParams(
            collective_id=0, has_side_effects=True, vmem_limit_bytes=58 * 2**20
        ),
    )(ids, weight, valid[0], out_grad[0], gate_pre[0], up_pre[0], w_gate[0], w_up[0], w_down[0])
    return out[None]


def solution(mesh):
    placed = (
        P("pipe", None, "expert", None),
        P("pipe", None, "expert", None),
        P("pipe", None, "expert", None),
        P("pipe", None, "expert"),
        P("pipe", None, None, "expert"),
        P("pipe", None, None, "expert"),
        P("pipe", "expert", None),
        P("pipe", "expert", None),
        P("pipe", None, "expert"),
    )
    return jax.shard_map(
        body, mesh=mesh, in_specs=placed, out_specs=P("pipe", None, "expert", None), check_vma=False
    )
```

```python
import jax
import jax.numpy as jnp
from jax import lax
from jax.experimental import pallas as pl
from jax.experimental.pallas import tpu as pltpu
from jax.sharding import PartitionSpec as P

EXPERTS = 8
MEMBERS = 8
CAP = 9
TOK = 64
LANES = 128
CHUNKS = 7
SLICE = CHUNKS * LANES
BLOCK = 64
SOURCES = 16
GROUP_ROWS = SOURCES * CAP
STACK = CHUNKS * GROUP_ROWS
ZONES = 4
HALVES = (((0, 0), (0, 1)), ((2, 0), (2, 1)), ((1, 0), (3, 0)), ((1, 1), (3, 1)))
GATE = (0, 3)
UP = (1, 2)
MESH = pl.DeviceIdType.MESH
F32 = jnp.float32
BF16 = jnp.bfloat16


def dot(a, b):
    return jnp.dot(a, b, preferred_element_type=F32)


def dot_t(a, b):
    return lax.dot_general(a, b, (((1,), (1,)), ((), ())), preferred_element_type=F32)


def iota(shape, axis):
    return lax.broadcasted_iota(jnp.int32, shape, axis)


def as_one(mask):
    return jnp.where(mask, 1.0, 0.0).astype(BF16)


def loop(count, step):
    def run(i, carry):
        step(i)
        return carry

    lax.fori_loop(0, count, run, 0)


def selection(ids):
    wide = 8 * TOK
    ahead = as_one(iota((TOK, TOK), 0) < iota((TOK, TOK), 1))
    named = jnp.where(ids == iota((EXPERTS, TOK), 0), 1.0, 0.0)
    slot = jnp.sum(named * dot(named.astype(BF16), ahead), axis=0, keepdims=True)
    line = iota((EXPERTS, TOK), 0)
    both = jnp.where(line == 0, ids.astype(F32), jnp.where(line == 1, slot, 0.0)).astype(BF16)
    col = iota((TOK, wide), 1)
    spread = dot(both, as_one((col & (TOK - 1)) == iota((TOK, wide), 0))).astype(jnp.int32)
    chunk = iota((1, wide), 1) >> 6
    target = spread[0:1] * BLOCK + chunk * CAP + spread[1:2]
    target = jnp.where(chunk < CHUNKS, target, -1)
    return jnp.where(iota((wide, wide), 0) == target, 1.0, 0.0)


def kernel(
    ids_ref,
    weight_ref,
    valid_ref,
    x_hbm,
    gate_hbm,
    up_hbm,
    wg_hbm,
    wu_hbm,
    wd_hbm,
    out_ref,
    x_ref,
    gate_ref,
    up_ref,
    wg_ref,
    wu_ref,
    wd_ref,
    sel_ref,
    back_ref,
    ids_out,
    ids_in,
    pack_ref,
    unpack_ref,
    scaled_ref,
    send_ref,
    recv_ref,
    rows_ref,
    part_ref,
    xin_ref,
    own_ref,
    sum_ref,
    yin_ref,
    grads_ref,
    ret_ref,
    home_ref,
    w_sem,
    ids_send,
    ids_recv,
    d_send,
    d_recv,
    d_local,
    x_send,
    x_recv,
    s_send,
    s_recv,
    g_send,
    g_recv,
    r_send,
    r_recv,
):
    p = lax.axis_index("pipe")
    me = lax.axis_index("expert")
    pipes = lax.axis_size("pipe")
    count = lax.axis_size("expert")
    group, member = me // MEMBERS, lax.rem(me, MEMBERS)
    first = group * MEMBERS
    z, half, y = me // SOURCES, member // 4, lax.rem(member, 4)
    other, spot = lax.rem(member + 4, MEMBERS), lax.rem(me, SOURCES)
    right, left = half * 4 + lax.rem(y + 1, 4), half * 4 + lax.rem(y + 3, 4)
    has_low, has_high = p > 0, p < pipes - 1
    low, high = jnp.maximum(p - 1, 0), jnp.minimum(p + 1, pipes - 1)

    onward = ((has_low, low), (has_high, high))

    tokens = pltpu.make_async_copy(x_hbm, x_ref, w_sem.at[0])
    tokens.start()
    barrier = pltpu.get_barrier_semaphore()

    def greet(i):
        pl.semaphore_signal(
            barrier, inc=1, device_id=(p, lax.rem(me + 1 + i, count)), device_id_type=MESH
        )

    loop(count - 1, greet)

    @pl.when(has_low)
    def _():
        pl.semaphore_signal(barrier, inc=1, device_id=(low, me), device_id_type=MESH)

    @pl.when(has_high)
    def _():
        pl.semaphore_signal(barrier, inc=1, device_id=(high, me), device_id_type=MESH)

    weights = [
        pltpu.make_async_copy(wd_hbm, wd_ref, w_sem.at[1]),
        pltpu.make_async_copy(wg_hbm, wg_ref, w_sem.at[2]),
        pltpu.make_async_copy(wu_hbm, wu_ref, w_sem.at[3]),
        pltpu.make_async_copy(gate_hbm, gate_ref, w_sem.at[4]),
        pltpu.make_async_copy(up_hbm, up_ref, w_sem.at[5]),
    ]
    for copy in weights:
        copy.start()

    def remote(src, dst, send, recv, device):
        return pltpu.make_async_remote_copy(
            src_ref=src,
            dst_ref=dst,
            send_sem=send,
            recv_sem=recv,
            device_id=device,
            device_id_type=MESH,
        )

    def drain(ref, sem):
        pltpu.make_async_copy(ref, ref, sem).wait()

    def zone_of(k):
        return lax.rem(z + k, ZONES)

    for m in range(2):
        ids = ids_ref[m]
        sel_ref[m] = selection(ids).astype(BF16)
        ids_out[m] = jnp.broadcast_to(
            jnp.concatenate([ids, jnp.zeros_like(ids)], axis=1), (EXPERTS, LANES)
        )

    tokens.wait()
    for m in range(2):
        same = iota((TOK, TOK), 0) == iota((TOK, TOK), 1)
        scale = weight_ref[m] * valid_ref[m : m + 1].astype(F32)
        scale = jnp.sum(jnp.where(same, scale, 0.0), axis=1, keepdims=True)
        for j in range(CHUNKS):
            for s in range(MEMBERS):
                col = s * SLICE + j * LANES
                scaled_ref[m, s // 2, TOK * j : TOK * (j + 1), LANES * (s % 2) : LANES * (s % 2 + 1)] = (
                    x_ref[m, :, col : col + LANES].astype(F32) * scale
                ).astype(BF16)

    def form(k):
        zone = zone_of(k)

        def part(i):
            m, pair = i // 4, lax.rem(i, 4)
            rows = pl.ds(pl.multiple_of(zone * 2 * BLOCK, 2 * BLOCK), 2 * BLOCK)
            o = dot(sel_ref[m, rows, 0 : CHUNKS * TOK], scaled_ref[m, pair]).astype(BF16)
            for e in range(2):
                for k in range(2):
                    send_ref[zone * SOURCES + e * MEMBERS + 2 * pair + k, m] = o[
                        BLOCK * e : BLOCK * (e + 1), LANES * k : LANES * (k + 1)
                    ]

        loop(8, part)

    def dispatch(c):
        if c < 2:
            zone = zone_of(HALVES[c][0][0])
            skip = 1 if c == 0 else 0

            def go(i):
                t = lax.rem(spot + skip + i, SOURCES)
                d = zone * SOURCES + t
                remote(send_ref.at[d], recv_ref.at[c, spot], d_send.at[c], d_recv.at[c], (p, d)).start()

            loop(SOURCES - skip, go)
            if c == 0:
                pltpu.make_async_copy(send_ref.at[me], recv_ref.at[0, spot], d_local).start()
            return

        def go(i):
            t = lax.rem(spot + i, SOURCES)
            for h, (back, m) in enumerate(HALVES[c]):
                d = zone_of(ZONES - back) * SOURCES + t
                remote(
                    send_ref.at[d, m], recv_ref.at[c, spot, h], d_send.at[c], d_recv.at[c], (p, d)
                ).start()

        loop(SOURCES, go)

    def hidden(c):
        if c == 0:
            drain(recv_ref.at[c, pl.ds(0, SOURCES - 1)], d_recv.at[c])
            drain(recv_ref.at[c, 0], d_local)
        else:
            drain(recv_ref.at[c], d_recv.at[c])
        both = [recv_ref[c, :, h].reshape(SOURCES * BLOCK, LANES) for h in range(2)]
        rows = dot(pack_ref[...], jnp.concatenate(both, axis=1)).astype(BF16)
        for m in range(2):
            for j in range(CHUNKS):
                rows_ref[GROUP_ROWS * m : GROUP_ROWS * (m + 1), LANES * j : LANES * (j + 1)] = rows[
                    GROUP_ROWS * j : GROUP_ROWS * (j + 1), LANES * m : LANES * (m + 1)
                ]

        def product(pair):
            w = wd_ref[pl.ds(pl.multiple_of(pair * 256, 256), 256), :]
            return dot_t(rows_ref[...], w)

        def give(i):
            o = product(2 * (1 - half) + i).astype(BF16)
            for k in range(2):
                part_ref[c, 2 * i + k] = o[:, LANES * k : LANES * (k + 1)]
            two = pl.ds(2 * i, 2)
            remote(
                part_ref.at[c, two], xin_ref.at[c, two], x_send.at[c], x_recv.at[c], (p, first + other)
            ).start()

        loop(2, give)

        def keep(i):
            o = product(2 * half + i)
            for k in range(2):
                own_ref[c, 2 * i + k] = o[:, LANES * k : LANES * (k + 1)]

        loop(2, keep)

    def reduce_x(c):
        drain(xin_ref.at[c], x_recv.at[c])

        def part(k):
            t = lax.rem(y + k, 4)
            o = own_ref[c, t] + xin_ref[c, t].astype(F32)

            @pl.when(k > 0)
            def _():
                sum_ref[c, t] = o.astype(BF16)
                remote(
                    sum_ref.at[c, t],
                    yin_ref.at[c, k - 1],
                    s_send.at[c],
                    s_recv.at[c],
                    (p, first + half * 4 + t),
                ).start()

            @pl.when(k == 0)
            def _():
                own_ref[c, t] = o

        loop(4, lambda i: part(lax.rem(i + 2, 4)))

    def activation(c):
        drain(yin_ref.at[c], s_recv.at[c])
        for h, (back, m) in enumerate(HALVES[c]):
            at = pl.ds(GROUP_ROWS * h, GROUP_ROWS)
            saved = pl.ds(pl.multiple_of(zone_of(back) * GROUP_ROWS, 16), GROUP_ROWS)
            o = own_ref[c, y, at, :]
            for k in range(3):
                o = o + yin_ref[c, k, at, :].astype(F32)
            g = gate_ref[m, saved, :].astype(F32)
            u = up_ref[m, saved, :].astype(F32)
            sig = jax.nn.sigmoid(g)
            grads_ref[c, member, GATE[h]] = (o * u * sig * (1.0 + g * (1.0 - sig))).astype(BF16)
            grads_ref[c, member, UP[h]] = (o * g * sig).astype(BF16)
        share(c, 0, other, member, 0, 3)
        share(c, 1, right, member, 0, 4)
        share(c, 1, left, member, 0, 4)

    def share(c, slot, to, whose, start, size):
        block = grads_ref.at[c, whose, pl.ds(start, size)]
        remote(block, block, g_send.at[c, slot], g_recv.at[c, slot], (p, first + to)).start()

    def arrived(c, slot, quarters):
        drain(grads_ref.at[c, 0, pl.ds(0, quarters)], g_recv.at[c, slot])

    def pass_on(c):
        drain(grads_ref.at[c, 0, pl.ds(0, 3)], g_recv.at[c, 0])
        share(c, 2, right, other, 0, 3)
        share(c, 2, left, other, 0, 3)
        drain(grads_ref.at[c, pl.ds(0, 2)], g_recv.at[c, 1])
        share(c, 3, left, right, 0, 2)
        share(c, 3, right, left, 2, 2)

    def pass_far(c):
        drain(grads_ref.at[c, 0], g_recv.at[c, 3])
        block = grads_ref.at[c, pl.ds(half * 4, 4), 3]
        remote(block, block, g_send.at[c, 5], g_recv.at[c, 5], (p, first + other)).start()
        drain(grads_ref.at[c, pl.ds(0, 2), pl.ds(0, 3)], g_recv.at[c, 2])
        over_right = lax.rem(right + 4, MEMBERS)
        over_left = lax.rem(left + 4, MEMBERS)
        one, two = (left, right) if c % 2 == 0 else (right, left)
        over_one, over_two = (over_left, over_right) if c % 2 == 0 else (over_right, over_left)
        share(c, 4, one, over_two, 0, 2)
        share(c, 4, two, over_one, 2, 1)

    def rows_out(c):
        drain(grads_ref.at[c, 0, pl.ds(0, 3)], g_recv.at[c, 4])
        drain(grads_ref.at[c, pl.ds(0, 4), 0], g_recv.at[c, 5])

        def whole(quarters):
            rows = [
                jnp.concatenate([grads_ref[c, k, q] for k in range(MEMBERS)], axis=1)
                for q in quarters
            ]
            return jnp.concatenate(rows, axis=0)

        gate, up = whole(GATE), whole(UP)
        r = (dot_t(gate, wg_ref[...]) + dot_t(up, wu_ref[...])).astype(BF16)
        r = jnp.concatenate(
            [
                jnp.concatenate(
                    [
                        r[GROUP_ROWS * m : GROUP_ROWS * (m + 1), LANES * j : LANES * (j + 1)]
                        for m in range(2)
                    ],
                    axis=1,
                )
                for j in range(CHUNKS)
            ],
            axis=0,
        )
        r = dot(unpack_ref[...], r).astype(BF16)
        for h, (back, m) in enumerate(HALVES[c]):
            ret_ref[c, h] = r[:, LANES * h : LANES * (h + 1)].reshape(SOURCES, BLOCK, LANES)
            zone = zone_of(back)

            @pl.when(onward[m][0])
            def _():
                def go(i):
                    t = lax.rem(spot + i, SOURCES)
                    remote(
                        ret_ref.at[c, h, t],
                        home_ref.at[m, me],
                        r_send.at[m],
                        r_recv.at[m],
                        (onward[m][1], zone * SOURCES + t),
                    ).start()

                loop(SOURCES, go)

    def selections():
        @pl.when(has_high)
        def _():
            drain(ids_in.at[0], ids_recv.at[0])
            back_ref[0] = selection(ids_in[0, 0:1, 0:TOK]).T.astype(BF16)

        @pl.when(has_low)
        def _():
            drain(ids_in.at[1], ids_recv.at[1])
            back_ref[1] = selection(ids_in[1, 0:1, 0:TOK]).T.astype(BF16)

    def finish(m, wanted):
        @pl.when(wanted)
        def _():
            drain(home_ref.at[m], r_recv.at[m])

            def part(i):
                blocks = [
                    jnp.concatenate([home_ref[m, e * MEMBERS + 2 * i + k] for k in range(2)], axis=1)
                    for e in range(EXPERTS)
                ]
                o = dot(back_ref[m, 0 : CHUNKS * TOK], jnp.concatenate(blocks, axis=0)).astype(BF16)
                for k in range(2):
                    for j in range(CHUNKS):
                        col = pl.multiple_of((2 * i + k) * SLICE + LANES * j, LANES)
                        out_ref[m, :, pl.ds(col, LANES)] = o[
                            TOK * j : TOK * (j + 1), LANES * k : LANES * (k + 1)
                        ]

            loop(4, part)

        @pl.when(jnp.logical_not(wanted))
        def _():
            out_ref[m] = jnp.zeros(out_ref.shape[1:], BF16)

    def build_pack():
        k = lax.rem(iota((1, SOURCES * BLOCK), 1), BLOCK)
        s = iota((1, SOURCES * BLOCK), 1) >> 6
        j = (k * 57) >> 9
        place = jnp.where(k < CHUNKS * CAP, j * GROUP_ROWS + s * CAP + k - j * CAP, -1)

        def part(i):
            at = pl.multiple_of(i * GROUP_ROWS, 16)
            shape = (GROUP_ROWS, SOURCES * BLOCK)
            pack_ref[pl.ds(at, GROUP_ROWS), :] = as_one(iota(shape, 0) + at == place)

        loop(CHUNKS, part)

    def build_unpack():
        r = iota((1, STACK), 1)
        j = jnp.zeros_like(r)
        for i in range(1, CHUNKS):
            j = j + jnp.where(r >= i * GROUP_ROWS, 1, 0)
        r = r - j * GROUP_ROWS
        s = (r * 57) >> 9
        origin = s * BLOCK + j * CAP + r - s * CAP

        def part(i):
            at = pl.multiple_of(i * 128, 128)
            unpack_ref[pl.ds(at, 128), :] = as_one(iota((128, STACK), 0) + at == origin)

        loop(SOURCES * BLOCK // 128, part)

    form(2)
    pl.semaphore_wait(
        barrier, count - 1 + jnp.where(has_low, 1, 0) + jnp.where(has_high, 1, 0)
    )
    dispatch(1)
    form(0)
    dispatch(0)
    form(1)
    form(3)
    dispatch(2)
    dispatch(3)

    to_low = remote(ids_out.at[0], ids_in.at[0], ids_send.at[0], ids_recv.at[0], (low, me))
    to_high = remote(ids_out.at[1], ids_in.at[1], ids_send.at[1], ids_recv.at[1], (high, me))

    @pl.when(has_low)
    def _():
        to_low.start()

    @pl.when(has_high)
    def _():
        to_high.start()

    build_pack()
    weights[0].wait()
    weights[3].wait()
    weights[4].wait()
    hidden(0)
    reduce_x(0)
    activation(0)
    hidden(1)
    pass_on(0)
    reduce_x(1)
    hidden(2)
    pass_far(0)
    activation(1)
    build_unpack()
    reduce_x(2)
    pass_on(1)
    hidden(3)
    activation(2)
    pass_far(1)
    weights[1].wait()
    weights[2].wait()
    reduce_x(3)
    pass_on(2)
    rows_out(1)
    activation(3)
    pass_far(2)
    selections()
    pass_on(3)
    rows_out(2)
    pass_far(3)
    rows_out(0)
    rows_out(3)
    finish(0, has_high)
    finish(1, has_low)

    @pl.when(has_low)
    def _():
        drain(ids_in.at[0], ids_send.at[0])
        drain(home_ref.at[0], r_send.at[0])

    @pl.when(has_high)
    def _():
        drain(ids_in.at[1], ids_send.at[1])
        drain(home_ref.at[1], r_send.at[1])

    for c in range(ZONES):
        drain(recv_ref.at[c, pl.ds(0, SOURCES - (1 if c == 0 else 0))], d_send.at[c])
        drain(xin_ref.at[c], x_send.at[c])
        drain(yin_ref.at[c], s_send.at[c])
        drain(grads_ref.at[c, 0, pl.ds(0, 3)], g_send.at[c, 0])
        drain(grads_ref.at[c, pl.ds(0, 2)], g_send.at[c, 1])
        drain(grads_ref.at[c, pl.ds(0, 2), pl.ds(0, 3)], g_send.at[c, 2])
        drain(grads_ref.at[c, 0], g_send.at[c, 3])
        drain(grads_ref.at[c, 0, pl.ds(0, 3)], g_send.at[c, 4])
        drain(grads_ref.at[c, pl.ds(0, 4), 0], g_send.at[c, 5])


def body(out_grad, expert_ids, gate_weights, valid, gate_pre, up_pre, w_gate, w_up, w_down):
    count = lax.axis_size("expert")
    ids = expert_ids.reshape(2, 1, TOK)
    weight = gate_weights.reshape(2, 1, TOK)
    vmem = pl.BlockSpec(memory_space=pltpu.VMEM)
    hbm = pl.BlockSpec(memory_space=pl.ANY)
    dma = pltpu.SemaphoreType.DMA
    out = pl.pallas_call(
        kernel,
        out_shape=jax.ShapeDtypeStruct(out_grad.shape[1:], BF16),
        in_specs=[vmem] * 3 + [hbm] * 6,
        out_specs=vmem,
        scratch_shapes=[
            pltpu.VMEM(out_grad.shape[1:], BF16),
            pltpu.VMEM(gate_pre.shape[1:], BF16),
            pltpu.VMEM(up_pre.shape[1:], BF16),
            pltpu.VMEM(w_gate.shape[1:], BF16),
            pltpu.VMEM(w_up.shape[1:], BF16),
            pltpu.VMEM(w_down.shape[1:], BF16),
            pltpu.VMEM((2, EXPERTS * BLOCK, 8 * TOK), BF16),
            pltpu.VMEM((2, 8 * TOK, EXPERTS * BLOCK), BF16),
            pltpu.VMEM((2, EXPERTS, LANES), jnp.int32),
            pltpu.VMEM((2, EXPERTS, LANES), jnp.int32),
            pltpu.VMEM((STACK, SOURCES * BLOCK), BF16),
            pltpu.VMEM((SOURCES * BLOCK, STACK), BF16),
            pltpu.VMEM((2, 4, CHUNKS * TOK, 2 * LANES), BF16),
            pltpu.VMEM((count, 2, BLOCK, LANES), BF16),
            pltpu.VMEM((ZONES, SOURCES, 2, BLOCK, LANES), BF16),
            pltpu.VMEM((2 * GROUP_ROWS, SLICE), BF16),
            pltpu.VMEM((ZONES, 4, 2 * GROUP_ROWS, LANES), BF16),
            pltpu.VMEM((ZONES, 4, 2 * GROUP_ROWS, LANES), BF16),
            pltpu.VMEM((ZONES, 4, 2 * GROUP_ROWS, LANES), F32),
            pltpu.VMEM((ZONES, 4, 2 * GROUP_ROWS, LANES), BF16),
            pltpu.VMEM((ZONES, 3, 2 * GROUP_ROWS, LANES), BF16),
            pltpu.VMEM((ZONES, MEMBERS, 4, GROUP_ROWS, LANES), BF16),
            pltpu.VMEM((ZONES, 2, SOURCES, BLOCK, LANES), BF16),
            pltpu.VMEM((2, count, BLOCK, LANES), BF16),
            dma((6,)),
            dma((2,)),
            dma((2,)),
            dma((ZONES,)),
            dma((ZONES,)),
            dma,
            dma((ZONES,)),
            dma((ZONES,)),
            dma((ZONES,)),
            dma((ZONES,)),
            dma((ZONES, 6)),
            dma((ZONES, 6)),
            dma((2,)),
            dma((2,)),
        ],
        compiler_params=pltpu.CompilerParams(
            collective_id=0, has_side_effects=True, vmem_limit_bytes=58 * 2**20
        ),
    )(ids, weight, valid[0], out_grad[0], gate_pre[0], up_pre[0], w_gate[0], w_up[0], w_down[0])
    return out[None]


def solution(mesh):
    placed = (
        P("pipe", None, "expert", None),
        P("pipe", None, "expert", None),
        P("pipe", None, "expert", None),
        P("pipe", None, "expert"),
        P("pipe", None, None, "expert"),
        P("pipe", None, None, "expert"),
        P("pipe", "expert", None),
        P("pipe", "expert", None),
        P("pipe", None, "expert"),
    )
    return jax.shard_map(
        body, mesh=mesh, in_specs=placed, out_specs=P("pipe", None, "expert", None), check_vma=False
    )
```

```python
import jax
import jax.numpy as jnp
from jax import lax
from jax.experimental import pallas as pl
from jax.experimental.pallas import tpu as pltpu
from jax.sharding import PartitionSpec as P

EXPERTS = 8
MEMBERS = 8
CAP = 9
TOK = 64
LANES = 128
CHUNKS = 7
SLICE = CHUNKS * LANES
BLOCK = 64
SOURCES = 16
GROUP_ROWS = SOURCES * CAP
STACK = CHUNKS * GROUP_ROWS
ZONES = 4
HALVES = (((0, 0), (0, 1)), ((2, 0), (2, 1)), ((1, 0), (3, 0)), ((1, 1), (3, 1)))
GATE = (0, 3)
UP = (1, 2)
MESH = pl.DeviceIdType.MESH
F32 = jnp.float32
BF16 = jnp.bfloat16


def dot(a, b):
    return jnp.dot(a, b, preferred_element_type=F32)


def dot_t(a, b):
    return lax.dot_general(a, b, (((1,), (1,)), ((), ())), preferred_element_type=F32)


def iota(shape, axis):
    return lax.broadcasted_iota(jnp.int32, shape, axis)


def as_one(mask):
    return jnp.where(mask, 1.0, 0.0).astype(BF16)


def loop(count, step):
    def run(i, carry):
        step(i)
        return carry

    lax.fori_loop(0, count, run, 0)


def selection(ids):
    wide = 8 * TOK
    ahead = as_one(iota((TOK, TOK), 0) < iota((TOK, TOK), 1))
    named = jnp.where(ids == iota((EXPERTS, TOK), 0), 1.0, 0.0)
    slot = jnp.sum(named * dot(named.astype(BF16), ahead), axis=0, keepdims=True)
    line = iota((EXPERTS, TOK), 0)
    both = jnp.where(line == 0, ids.astype(F32), jnp.where(line == 1, slot, 0.0)).astype(BF16)
    col = iota((TOK, wide), 1)
    spread = dot(both, as_one((col & (TOK - 1)) == iota((TOK, wide), 0))).astype(jnp.int32)
    chunk = iota((1, wide), 1) >> 6
    target = spread[0:1] * BLOCK + chunk * CAP + spread[1:2]
    target = jnp.where(chunk < CHUNKS, target, -1)
    return jnp.where(iota((wide, wide), 0) == target, 1.0, 0.0)


def kernel(
    ids_ref,
    weight_ref,
    valid_ref,
    x_hbm,
    gate_hbm,
    up_hbm,
    wg_hbm,
    wu_hbm,
    wd_hbm,
    out_ref,
    x_ref,
    gate_ref,
    up_ref,
    wg_ref,
    wu_ref,
    wd_ref,
    sel_ref,
    back_ref,
    ids_out,
    ids_in,
    pack_ref,
    unpack_ref,
    scale_ref,
    send_ref,
    recv_ref,
    rows_ref,
    part_ref,
    xin_ref,
    own_ref,
    sum_ref,
    yin_ref,
    grads_ref,
    ret_ref,
    home_ref,
    w_sem,
    ids_send,
    ids_recv,
    d_send,
    d_recv,
    d_local,
    x_send,
    x_recv,
    s_send,
    s_recv,
    g_send,
    g_recv,
    r_send,
    r_recv,
):
    p = lax.axis_index("pipe")
    me = lax.axis_index("expert")
    pipes = lax.axis_size("pipe")
    count = lax.axis_size("expert")
    group, member = me // MEMBERS, lax.rem(me, MEMBERS)
    first = group * MEMBERS
    z, half, y = me // SOURCES, member // 4, lax.rem(member, 4)
    other, spot = lax.rem(member + 4, MEMBERS), lax.rem(me, SOURCES)
    right, left = half * 4 + lax.rem(y + 1, 4), half * 4 + lax.rem(y + 3, 4)
    has_low, has_high = p > 0, p < pipes - 1
    low, high = jnp.maximum(p - 1, 0), jnp.minimum(p + 1, pipes - 1)

    onward = ((has_low, low), (has_high, high))

    tokens = pltpu.make_async_copy(x_hbm, x_ref, w_sem.at[0])
    tokens.start()
    barrier = pltpu.get_barrier_semaphore()

    def greet(i):
        pl.semaphore_signal(
            barrier, inc=1, device_id=(p, lax.rem(me + 1 + i, count)), device_id_type=MESH
        )

    loop(count - 1, greet)

    @pl.when(has_low)
    def _():
        pl.semaphore_signal(barrier, inc=1, device_id=(low, me), device_id_type=MESH)

    @pl.when(has_high)
    def _():
        pl.semaphore_signal(barrier, inc=1, device_id=(high, me), device_id_type=MESH)

    weights = [
        pltpu.make_async_copy(wd_hbm, wd_ref, w_sem.at[1]),
        pltpu.make_async_copy(wg_hbm, wg_ref, w_sem.at[2]),
        pltpu.make_async_copy(wu_hbm, wu_ref, w_sem.at[3]),
        pltpu.make_async_copy(gate_hbm, gate_ref, w_sem.at[4]),
        pltpu.make_async_copy(up_hbm, up_ref, w_sem.at[5]),
    ]
    for copy in weights:
        copy.start()

    def remote(src, dst, send, recv, device):
        return pltpu.make_async_remote_copy(
            src_ref=src,
            dst_ref=dst,
            send_sem=send,
            recv_sem=recv,
            device_id=device,
            device_id_type=MESH,
        )

    def drain(ref, sem):
        pltpu.make_async_copy(ref, ref, sem).wait()

    def zone_of(k):
        return lax.rem(z + k, ZONES)

    for m in range(2):
        ids = ids_ref[m]
        sel = selection(ids)
        sel_ref[m] = sel.astype(BF16)
        ids_out[m] = jnp.broadcast_to(
            jnp.concatenate([ids, jnp.zeros_like(ids)], axis=1), (EXPERTS, LANES)
        )
        scale = weight_ref[m] * valid_ref[m : m + 1].astype(F32)
        scale = jnp.concatenate([scale] * 8, axis=1)
        scale_ref[m] = jnp.sum(sel * scale, axis=1, keepdims=True)
    tokens.wait()

    def form(k):
        zone = zone_of(k)

        def part(i):
            m, pair = i // 4, lax.rem(i, 4)
            rows = pl.ds(pl.multiple_of(zone * 2 * BLOCK, 2 * BLOCK), 2 * BLOCK)
            x = [
                jnp.concatenate(
                    [
                        x_ref[m, :, pl.ds(pl.multiple_of((2 * pair + k) * SLICE, LANES) + LANES * j, LANES)]
                        for k in range(2)
                    ],
                    axis=1,
                )
                for j in range(CHUNKS)
            ]
            o = dot(sel_ref[m, rows, 0 : CHUNKS * TOK], jnp.concatenate(x, axis=0))
            o = (o * scale_ref[m, rows, :]).astype(BF16)
            for e in range(2):
                for k in range(2):
                    send_ref[zone * SOURCES + e * MEMBERS + 2 * pair + k, m] = o[
                        BLOCK * e : BLOCK * (e + 1), LANES * k : LANES * (k + 1)
                    ]

        loop(8, part)

    def dispatch(c):
        if c < 2:
            zone = zone_of(HALVES[c][0][0])
            skip = 1 if c == 0 else 0

            def go(i):
                t = lax.rem(spot + skip + i, SOURCES)
                d = zone * SOURCES + t
                remote(send_ref.at[d], recv_ref.at[c, spot], d_send.at[c], d_recv.at[c], (p, d)).start()

            loop(SOURCES - skip, go)
            if c == 0:
                pltpu.make_async_copy(send_ref.at[me], recv_ref.at[0, spot], d_local).start()
            return

        def go(i):
            t = lax.rem(spot + i, SOURCES)
            for h, (back, m) in enumerate(HALVES[c]):
                d = zone_of(ZONES - back) * SOURCES + t
                remote(
                    send_ref.at[d, m], recv_ref.at[c, spot, h], d_send.at[c], d_recv.at[c], (p, d)
                ).start()

        loop(SOURCES, go)

    def hidden(c):
        if c == 0:
            drain(recv_ref.at[c, pl.ds(0, SOURCES - 1)], d_recv.at[c])
            drain(recv_ref.at[c, 0], d_local)
        else:
            drain(recv_ref.at[c], d_recv.at[c])
        both = [recv_ref[c, :, h].reshape(SOURCES * BLOCK, LANES) for h in range(2)]
        rows = dot(pack_ref[...], jnp.concatenate(both, axis=1)).astype(BF16)
        for m in range(2):
            for j in range(CHUNKS):
                rows_ref[GROUP_ROWS * m : GROUP_ROWS * (m + 1), LANES * j : LANES * (j + 1)] = rows[
                    GROUP_ROWS * j : GROUP_ROWS * (j + 1), LANES * m : LANES * (m + 1)
                ]

        def product(pair):
            w = wd_ref[pl.ds(pl.multiple_of(pair * 256, 256), 256), :]
            return dot_t(rows_ref[...], w)

        def give(i):
            o = product(2 * (1 - half) + i).astype(BF16)
            for k in range(2):
                part_ref[c, 2 * i + k] = o[:, LANES * k : LANES * (k + 1)]
            two = pl.ds(2 * i, 2)
            remote(
                part_ref.at[c, two], xin_ref.at[c, two], x_send.at[c], x_recv.at[c], (p, first + other)
            ).start()

        loop(2, give)

        def keep(i):
            o = product(2 * half + i)
            for k in range(2):
                own_ref[c, 2 * i + k] = o[:, LANES * k : LANES * (k + 1)]

        loop(2, keep)

    def reduce_x(c):
        drain(xin_ref.at[c], x_recv.at[c])

        def part(k):
            t = lax.rem(y + k, 4)
            o = own_ref[c, t] + xin_ref[c, t].astype(F32)

            @pl.when(k > 0)
            def _():
                sum_ref[c, t] = o.astype(BF16)
                remote(
                    sum_ref.at[c, t],
                    yin_ref.at[c, k - 1],
                    s_send.at[c],
                    s_recv.at[c],
                    (p, first + half * 4 + t),
                ).start()

            @pl.when(k == 0)
            def _():
                own_ref[c, t] = o

        loop(4, lambda i: part(lax.rem(i + 2, 4)))

    def activation(c):
        drain(yin_ref.at[c], s_recv.at[c])
        for h, (back, m) in enumerate(HALVES[c]):
            at = pl.ds(GROUP_ROWS * h, GROUP_ROWS)
            saved = pl.ds(pl.multiple_of(zone_of(back) * GROUP_ROWS, 16), GROUP_ROWS)
            o = own_ref[c, y, at, :]
            for k in range(3):
                o = o + yin_ref[c, k, at, :].astype(F32)
            g = gate_ref[m, saved, :].astype(F32)
            u = up_ref[m, saved, :].astype(F32)
            sig = jax.nn.sigmoid(g)
            grads_ref[c, member, GATE[h]] = (o * u * sig * (1.0 + g * (1.0 - sig))).astype(BF16)
            grads_ref[c, member, UP[h]] = (o * g * sig).astype(BF16)
        share(c, 0, other, member, 0, 3)
        share(c, 1, right, member, 0, 4)
        share(c, 1, left, member, 0, 4)

    def share(c, slot, to, whose, start, size):
        block = grads_ref.at[c, whose, pl.ds(start, size)]
        remote(block, block, g_send.at[c, slot], g_recv.at[c, slot], (p, first + to)).start()

    def arrived(c, slot, quarters):
        drain(grads_ref.at[c, 0, pl.ds(0, quarters)], g_recv.at[c, slot])

    def pass_on(c):
        drain(grads_ref.at[c, 0, pl.ds(0, 3)], g_recv.at[c, 0])
        share(c, 2, right, other, 0, 3)
        share(c, 2, left, other, 0, 3)
        drain(grads_ref.at[c, pl.ds(0, 2)], g_recv.at[c, 1])
        share(c, 3, left, right, 0, 2)
        share(c, 3, right, left, 2, 2)

    def pass_far(c):
        drain(grads_ref.at[c, 0], g_recv.at[c, 3])
        block = grads_ref.at[c, pl.ds(half * 4, 4), 3]
        remote(block, block, g_send.at[c, 5], g_recv.at[c, 5], (p, first + other)).start()
        drain(grads_ref.at[c, pl.ds(0, 2), pl.ds(0, 3)], g_recv.at[c, 2])
        over_right = lax.rem(right + 4, MEMBERS)
        over_left = lax.rem(left + 4, MEMBERS)
        one, two = (left, right) if c % 2 == 0 else (right, left)
        over_one, over_two = (over_left, over_right) if c % 2 == 0 else (over_right, over_left)
        share(c, 4, one, over_two, 0, 2)
        share(c, 4, two, over_one, 2, 1)

    def rows_out(c):
        drain(grads_ref.at[c, 0, pl.ds(0, 3)], g_recv.at[c, 4])
        drain(grads_ref.at[c, pl.ds(0, 4), 0], g_recv.at[c, 5])

        def whole(quarters):
            rows = [
                jnp.concatenate([grads_ref[c, k, q] for k in range(MEMBERS)], axis=1)
                for q in quarters
            ]
            return jnp.concatenate(rows, axis=0)

        gate, up = whole(GATE), whole(UP)
        r = (dot_t(gate, wg_ref[...]) + dot_t(up, wu_ref[...])).astype(BF16)
        r = jnp.concatenate(
            [
                jnp.concatenate(
                    [
                        r[GROUP_ROWS * m : GROUP_ROWS * (m + 1), LANES * j : LANES * (j + 1)]
                        for m in range(2)
                    ],
                    axis=1,
                )
                for j in range(CHUNKS)
            ],
            axis=0,
        )
        r = dot(unpack_ref[...], r).astype(BF16)
        for h, (back, m) in enumerate(HALVES[c]):
            ret_ref[c, h] = r[:, LANES * h : LANES * (h + 1)].reshape(SOURCES, BLOCK, LANES)
            zone = zone_of(back)

            @pl.when(onward[m][0])
            def _():
                def go(i):
                    t = lax.rem(spot + i, SOURCES)
                    remote(
                        ret_ref.at[c, h, t],
                        home_ref.at[m, me],
                        r_send.at[m],
                        r_recv.at[m],
                        (onward[m][1], zone * SOURCES + t),
                    ).start()

                loop(SOURCES, go)

    def selections():
        @pl.when(has_high)
        def _():
            drain(ids_in.at[0], ids_recv.at[0])
            back_ref[0] = selection(ids_in[0, 0:1, 0:TOK]).T.astype(BF16)

        @pl.when(has_low)
        def _():
            drain(ids_in.at[1], ids_recv.at[1])
            back_ref[1] = selection(ids_in[1, 0:1, 0:TOK]).T.astype(BF16)

    def finish(m, wanted):
        @pl.when(wanted)
        def _():
            drain(home_ref.at[m], r_recv.at[m])

            def part(i):
                blocks = [
                    jnp.concatenate([home_ref[m, e * MEMBERS + 2 * i + k] for k in range(2)], axis=1)
                    for e in range(EXPERTS)
                ]
                o = dot(back_ref[m, 0 : CHUNKS * TOK], jnp.concatenate(blocks, axis=0)).astype(BF16)
                for k in range(2):
                    for j in range(CHUNKS):
                        col = pl.multiple_of((2 * i + k) * SLICE + LANES * j, LANES)
                        out_ref[m, :, pl.ds(col, LANES)] = o[
                            TOK * j : TOK * (j + 1), LANES * k : LANES * (k + 1)
                        ]

            loop(4, part)

        @pl.when(jnp.logical_not(wanted))
        def _():
            out_ref[m] = jnp.zeros(out_ref.shape[1:], BF16)

    def build_pack():
        k = lax.rem(iota((1, SOURCES * BLOCK), 1), BLOCK)
        s = iota((1, SOURCES * BLOCK), 1) >> 6
        j = (k * 57) >> 9
        place = jnp.where(k < CHUNKS * CAP, j * GROUP_ROWS + s * CAP + k - j * CAP, -1)

        def part(i):
            at = pl.multiple_of(i * GROUP_ROWS, 16)
            shape = (GROUP_ROWS, SOURCES * BLOCK)
            pack_ref[pl.ds(at, GROUP_ROWS), :] = as_one(iota(shape, 0) + at == place)

        loop(CHUNKS, part)

    def build_unpack():
        r = iota((1, STACK), 1)
        j = jnp.zeros_like(r)
        for i in range(1, CHUNKS):
            j = j + jnp.where(r >= i * GROUP_ROWS, 1, 0)
        r = r - j * GROUP_ROWS
        s = (r * 57) >> 9
        origin = s * BLOCK + j * CAP + r - s * CAP

        def part(i):
            at = pl.multiple_of(i * 128, 128)
            unpack_ref[pl.ds(at, 128), :] = as_one(iota((128, STACK), 0) + at == origin)

        loop(SOURCES * BLOCK // 128, part)

    form(2)
    pl.semaphore_wait(
        barrier, count - 1 + jnp.where(has_low, 1, 0) + jnp.where(has_high, 1, 0)
    )
    dispatch(1)
    form(0)
    dispatch(0)
    form(1)
    form(3)
    dispatch(2)
    dispatch(3)

    to_low = remote(ids_out.at[0], ids_in.at[0], ids_send.at[0], ids_recv.at[0], (low, me))
    to_high = remote(ids_out.at[1], ids_in.at[1], ids_send.at[1], ids_recv.at[1], (high, me))

    @pl.when(has_low)
    def _():
        to_low.start()

    @pl.when(has_high)
    def _():
        to_high.start()

    build_pack()
    weights[0].wait()
    weights[3].wait()
    weights[4].wait()
    hidden(0)
    reduce_x(0)
    activation(0)
    hidden(1)
    pass_on(0)
    hidden(2)
    reduce_x(1)
    pass_far(0)
    activation(1)
    build_unpack()
    hidden(3)
    reduce_x(2)
    pass_on(1)
    activation(2)
    pass_far(1)
    weights[1].wait()
    weights[2].wait()
    reduce_x(3)
    pass_on(2)
    rows_out(1)
    activation(3)
    pass_far(2)
    pass_on(3)
    selections()
    rows_out(2)
    pass_far(3)
    rows_out(0)
    rows_out(3)
    finish(0, has_high)
    finish(1, has_low)

    @pl.when(has_low)
    def _():
        drain(ids_in.at[0], ids_send.at[0])
        drain(home_ref.at[0], r_send.at[0])

    @pl.when(has_high)
    def _():
        drain(ids_in.at[1], ids_send.at[1])
        drain(home_ref.at[1], r_send.at[1])

    for c in range(ZONES):
        drain(recv_ref.at[c, pl.ds(0, SOURCES - (1 if c == 0 else 0))], d_send.at[c])
        drain(xin_ref.at[c], x_send.at[c])
        drain(yin_ref.at[c], s_send.at[c])
        drain(grads_ref.at[c, 0, pl.ds(0, 3)], g_send.at[c, 0])
        drain(grads_ref.at[c, pl.ds(0, 2)], g_send.at[c, 1])
        drain(grads_ref.at[c, pl.ds(0, 2), pl.ds(0, 3)], g_send.at[c, 2])
        drain(grads_ref.at[c, 0], g_send.at[c, 3])
        drain(grads_ref.at[c, 0, pl.ds(0, 3)], g_send.at[c, 4])
        drain(grads_ref.at[c, pl.ds(0, 4), 0], g_send.at[c, 5])


def body(out_grad, expert_ids, gate_weights, valid, gate_pre, up_pre, w_gate, w_up, w_down):
    count = lax.axis_size("expert")
    ids = expert_ids.reshape(2, 1, TOK)
    weight = gate_weights.reshape(2, 1, TOK)
    vmem = pl.BlockSpec(memory_space=pltpu.VMEM)
    hbm = pl.BlockSpec(memory_space=pl.ANY)
    dma = pltpu.SemaphoreType.DMA
    out = pl.pallas_call(
        kernel,
        out_shape=jax.ShapeDtypeStruct(out_grad.shape[1:], BF16),
        in_specs=[vmem] * 3 + [hbm] * 6,
        out_specs=vmem,
        scratch_shapes=[
            pltpu.VMEM(out_grad.shape[1:], BF16),
            pltpu.VMEM(gate_pre.shape[1:], BF16),
            pltpu.VMEM(up_pre.shape[1:], BF16),
            pltpu.VMEM(w_gate.shape[1:], BF16),
            pltpu.VMEM(w_up.shape[1:], BF16),
            pltpu.VMEM(w_down.shape[1:], BF16),
            pltpu.VMEM((2, EXPERTS * BLOCK, 8 * TOK), BF16),
            pltpu.VMEM((2, 8 * TOK, EXPERTS * BLOCK), BF16),
            pltpu.VMEM((2, EXPERTS, LANES), jnp.int32),
            pltpu.VMEM((2, EXPERTS, LANES), jnp.int32),
            pltpu.VMEM((STACK, SOURCES * BLOCK), BF16),
            pltpu.VMEM((SOURCES * BLOCK, STACK), BF16),
            pltpu.VMEM((2, EXPERTS * BLOCK, 1), F32),
            pltpu.VMEM((count, 2, BLOCK, LANES), BF16),
            pltpu.VMEM((ZONES, SOURCES, 2, BLOCK, LANES), BF16),
            pltpu.VMEM((2 * GROUP_ROWS, SLICE), BF16),
            pltpu.VMEM((ZONES, 4, 2 * GROUP_ROWS, LANES), BF16),
            pltpu.VMEM((ZONES, 4, 2 * GROUP_ROWS, LANES), BF16),
            pltpu.VMEM((ZONES, 4, 2 * GROUP_ROWS, LANES), F32),
            pltpu.VMEM((ZONES, 4, 2 * GROUP_ROWS, LANES), BF16),
            pltpu.VMEM((ZONES, 3, 2 * GROUP_ROWS, LANES), BF16),
            pltpu.VMEM((ZONES, MEMBERS, 4, GROUP_ROWS, LANES), BF16),
            pltpu.VMEM((ZONES, 2, SOURCES, BLOCK, LANES), BF16),
            pltpu.VMEM((2, count, BLOCK, LANES), BF16),
            dma((6,)),
            dma((2,)),
            dma((2,)),
            dma((ZONES,)),
            dma((ZONES,)),
            dma,
            dma((ZONES,)),
            dma((ZONES,)),
            dma((ZONES,)),
            dma((ZONES,)),
            dma((ZONES, 6)),
            dma((ZONES, 6)),
            dma((2,)),
            dma((2,)),
        ],
        compiler_params=pltpu.CompilerParams(
            collective_id=0, has_side_effects=True, vmem_limit_bytes=58 * 2**20
        ),
    )(ids, weight, valid[0], out_grad[0], gate_pre[0], up_pre[0], w_gate[0], w_up[0], w_down[0])
    return out[None]


def solution(mesh):
    placed = (
        P("pipe", None, "expert", None),
        P("pipe", None, "expert", None),
        P("pipe", None, "expert", None),
        P("pipe", None, "expert"),
        P("pipe", None, None, "expert"),
        P("pipe", None, None, "expert"),
        P("pipe", "expert", None),
        P("pipe", "expert", None),
        P("pipe", None, "expert"),
    )
    return jax.shard_map(
        body, mesh=mesh, in_specs=placed, out_specs=P("pipe", None, "expert", None), check_vma=False
    )
```

```python
import jax
import jax.numpy as jnp
from jax import lax
from jax.experimental import pallas as pl
from jax.experimental.pallas import tpu as pltpu
from jax.sharding import PartitionSpec as P

EXPERTS = 8
MEMBERS = 8
CAP = 9
TOK = 64
LANES = 128
CHUNKS = 7
SLICE = CHUNKS * LANES
BLOCK = 64
SOURCES = 16
GROUP_ROWS = SOURCES * CAP
STACK = CHUNKS * GROUP_ROWS
ZONES = 4
HALVES = (((0, 0), (0, 1)), ((2, 0), (2, 1)), ((1, 0), (3, 0)), ((1, 1), (3, 1)))
GATE = (0, 3)
UP = (1, 2)
MESH = pl.DeviceIdType.MESH
F32 = jnp.float32
BF16 = jnp.bfloat16


def dot(a, b):
    return jnp.dot(a, b, preferred_element_type=F32)


def dot_t(a, b):
    return lax.dot_general(a, b, (((1,), (1,)), ((), ())), preferred_element_type=F32)


def iota(shape, axis):
    return lax.broadcasted_iota(jnp.int32, shape, axis)


def as_one(mask):
    return jnp.where(mask, 1.0, 0.0).astype(BF16)


def loop(count, step):
    def run(i, carry):
        step(i)
        return carry

    lax.fori_loop(0, count, run, 0)


def selection(ids):
    wide = 8 * TOK
    ahead = as_one(iota((TOK, TOK), 0) < iota((TOK, TOK), 1))
    named = jnp.where(ids == iota((EXPERTS, TOK), 0), 1.0, 0.0)
    slot = jnp.sum(named * dot(named.astype(BF16), ahead), axis=0, keepdims=True)
    line = iota((EXPERTS, TOK), 0)
    both = jnp.where(line == 0, ids.astype(F32), jnp.where(line == 1, slot, 0.0)).astype(BF16)
    col = iota((TOK, wide), 1)
    spread = dot(both, as_one((col & (TOK - 1)) == iota((TOK, wide), 0))).astype(jnp.int32)
    chunk = iota((1, wide), 1) >> 6
    target = spread[0:1] * BLOCK + chunk * CAP + spread[1:2]
    target = jnp.where(chunk < CHUNKS, target, -1)
    return jnp.where(iota((wide, wide), 0) == target, 1.0, 0.0)


def kernel(
    ids_ref,
    weight_ref,
    valid_ref,
    x_hbm,
    gate_hbm,
    up_hbm,
    wg_hbm,
    wu_hbm,
    wd_hbm,
    out_ref,
    x_ref,
    gate_ref,
    up_ref,
    wg_ref,
    wu_ref,
    wd_ref,
    sel_ref,
    back_ref,
    ids_out,
    ids_in,
    pack_ref,
    unpack_ref,
    scale_ref,
    send_ref,
    recv_ref,
    rows_ref,
    part_ref,
    xin_ref,
    own_ref,
    sum_ref,
    yin_ref,
    grads_ref,
    ret_ref,
    home_ref,
    w_sem,
    ids_send,
    ids_recv,
    d_send,
    d_recv,
    d_local,
    x_send,
    x_recv,
    s_send,
    s_recv,
    g_send,
    g_recv,
    r_send,
    r_recv,
):
    p = lax.axis_index("pipe")
    me = lax.axis_index("expert")
    pipes = lax.axis_size("pipe")
    count = lax.axis_size("expert")
    group, member = me // MEMBERS, lax.rem(me, MEMBERS)
    first = group * MEMBERS
    z, half, y = me // SOURCES, member // 4, lax.rem(member, 4)
    other, spot = lax.rem(member + 4, MEMBERS), lax.rem(me, SOURCES)
    right, left = half * 4 + lax.rem(y + 1, 4), half * 4 + lax.rem(y + 3, 4)
    has_low, has_high = p > 0, p < pipes - 1
    low, high = jnp.maximum(p - 1, 0), jnp.minimum(p + 1, pipes - 1)

    onward = ((has_low, low), (has_high, high))

    tokens = pltpu.make_async_copy(x_hbm, x_ref, w_sem.at[0])
    tokens.start()
    barrier = pltpu.get_barrier_semaphore()

    def greet(i):
        pl.semaphore_signal(
            barrier, inc=1, device_id=(p, lax.rem(me + 1 + i, count)), device_id_type=MESH
        )

    loop(count - 1, greet)

    @pl.when(has_low)
    def _():
        pl.semaphore_signal(barrier, inc=1, device_id=(low, me), device_id_type=MESH)

    @pl.when(has_high)
    def _():
        pl.semaphore_signal(barrier, inc=1, device_id=(high, me), device_id_type=MESH)

    weights = [
        pltpu.make_async_copy(wd_hbm, wd_ref, w_sem.at[1]),
        pltpu.make_async_copy(wg_hbm, wg_ref, w_sem.at[2]),
        pltpu.make_async_copy(wu_hbm, wu_ref, w_sem.at[3]),
        pltpu.make_async_copy(gate_hbm, gate_ref, w_sem.at[4]),
        pltpu.make_async_copy(up_hbm, up_ref, w_sem.at[5]),
    ]
    for copy in weights:
        copy.start()

    def remote(src, dst, send, recv, device):
        return pltpu.make_async_remote_copy(
            src_ref=src,
            dst_ref=dst,
            send_sem=send,
            recv_sem=recv,
            device_id=device,
            device_id_type=MESH,
        )

    def drain(ref, sem):
        pltpu.make_async_copy(ref, ref, sem).wait()

    def zone_of(k):
        return lax.rem(z + k, ZONES)

    for m in range(2):
        ids = ids_ref[m]
        sel = selection(ids)
        sel_ref[m] = sel.astype(BF16)
        ids_out[m] = jnp.broadcast_to(
            jnp.concatenate([ids, jnp.zeros_like(ids)], axis=1), (EXPERTS, LANES)
        )
        scale = weight_ref[m] * valid_ref[m : m + 1].astype(F32)
        scale = jnp.concatenate([scale] * 8, axis=1)
        scale_ref[m] = jnp.sum(sel * scale, axis=1, keepdims=True)
    tokens.wait()

    def form(k):
        zone = zone_of(k)

        def part(i):
            m, pair = i // 4, lax.rem(i, 4)
            rows = pl.ds(pl.multiple_of(zone * 2 * BLOCK, 2 * BLOCK), 2 * BLOCK)
            x = [
                jnp.concatenate(
                    [
                        x_ref[m, :, pl.ds(pl.multiple_of((2 * pair + k) * SLICE, LANES) + LANES * j, LANES)]
                        for k in range(2)
                    ],
                    axis=1,
                )
                for j in range(CHUNKS)
            ]
            o = dot(sel_ref[m, rows, 0 : CHUNKS * TOK], jnp.concatenate(x, axis=0))
            o = (o * scale_ref[m, rows, :]).astype(BF16)
            for e in range(2):
                for k in range(2):
                    send_ref[zone * SOURCES + e * MEMBERS + 2 * pair + k, m] = o[
                        BLOCK * e : BLOCK * (e + 1), LANES * k : LANES * (k + 1)
                    ]

        loop(8, part)

    def dispatch(c):
        if c < 2:
            zone = zone_of(HALVES[c][0][0])
            skip = 1 if c == 0 else 0

            def go(i):
                t = lax.rem(spot + skip + i, SOURCES)
                d = zone * SOURCES + t
                remote(send_ref.at[d], recv_ref.at[c, spot], d_send.at[c], d_recv.at[c], (p, d)).start()

            loop(SOURCES - skip, go)
            if c == 0:
                pltpu.make_async_copy(send_ref.at[me], recv_ref.at[0, spot], d_local).start()
            return

        def go(i):
            t = lax.rem(spot + i, SOURCES)
            for h, (back, m) in enumerate(HALVES[c]):
                d = zone_of(ZONES - back) * SOURCES + t
                remote(
                    send_ref.at[d, m], recv_ref.at[c, spot, h], d_send.at[c], d_recv.at[c], (p, d)
                ).start()

        loop(SOURCES, go)

    def hidden(c):
        if c == 0:
            drain(recv_ref.at[c, pl.ds(0, SOURCES - 1)], d_recv.at[c])
            drain(recv_ref.at[c, 0], d_local)
        else:
            drain(recv_ref.at[c], d_recv.at[c])
        both = [recv_ref[c, :, h].reshape(SOURCES * BLOCK, LANES) for h in range(2)]
        rows = dot(pack_ref[...], jnp.concatenate(both, axis=1)).astype(BF16)
        for m in range(2):
            for j in range(CHUNKS):
                rows_ref[GROUP_ROWS * m : GROUP_ROWS * (m + 1), LANES * j : LANES * (j + 1)] = rows[
                    GROUP_ROWS * j : GROUP_ROWS * (j + 1), LANES * m : LANES * (m + 1)
                ]

        def product(pair):
            w = wd_ref[pl.ds(pl.multiple_of(pair * 256, 256), 256), :]
            return dot_t(rows_ref[...], w)

        def give(i):
            o = product(2 * (1 - half) + i).astype(BF16)
            for k in range(2):
                part_ref[c, 2 * i + k] = o[:, LANES * k : LANES * (k + 1)]
            two = pl.ds(2 * i, 2)
            remote(
                part_ref.at[c, two], xin_ref.at[c, two], x_send.at[c], x_recv.at[c], (p, first + other)
            ).start()

        loop(2, give)

        def keep(i):
            o = product(2 * half + i)
            for k in range(2):
                own_ref[c, 2 * i + k] = o[:, LANES * k : LANES * (k + 1)]

        loop(2, keep)

    def reduce_x(c):
        drain(xin_ref.at[c], x_recv.at[c])

        def part(k):
            t = lax.rem(y + k, 4)
            o = own_ref[c, t] + xin_ref[c, t].astype(F32)

            @pl.when(k > 0)
            def _():
                sum_ref[c, t] = o.astype(BF16)
                remote(
                    sum_ref.at[c, t],
                    yin_ref.at[c, k - 1],
                    s_send.at[c],
                    s_recv.at[c],
                    (p, first + half * 4 + t),
                ).start()

            @pl.when(k == 0)
            def _():
                own_ref[c, t] = o

        loop(4, lambda i: part(lax.rem(i + 2, 4)))

    def activation(c):
        drain(yin_ref.at[c], s_recv.at[c])
        for h, (back, m) in enumerate(HALVES[c]):
            at = pl.ds(GROUP_ROWS * h, GROUP_ROWS)
            saved = pl.ds(pl.multiple_of(zone_of(back) * GROUP_ROWS, 16), GROUP_ROWS)
            o = own_ref[c, y, at, :]
            for k in range(3):
                o = o + yin_ref[c, k, at, :].astype(F32)
            g = gate_ref[m, saved, :].astype(F32)
            u = up_ref[m, saved, :].astype(F32)
            sig = jax.nn.sigmoid(g)
            grads_ref[c, member, GATE[h]] = (o * u * sig * (1.0 + g * (1.0 - sig))).astype(BF16)
            grads_ref[c, member, UP[h]] = (o * g * sig).astype(BF16)
        share(c, 0, other, member, 0, 3)
        share(c, 1, right, member, 0, 4)
        share(c, 1, left, member, 0, 4)

    def share(c, slot, to, whose, start, size):
        block = grads_ref.at[c, whose, pl.ds(start, size)]
        remote(block, block, g_send.at[c, slot], g_recv.at[c, slot], (p, first + to)).start()

    def arrived(c, slot, quarters):
        drain(grads_ref.at[c, 0, pl.ds(0, quarters)], g_recv.at[c, slot])

    def pass_on(c):
        drain(grads_ref.at[c, 0, pl.ds(0, 3)], g_recv.at[c, 0])
        share(c, 2, right, other, 0, 3)
        share(c, 2, left, other, 0, 3)
        drain(grads_ref.at[c, pl.ds(0, 2)], g_recv.at[c, 1])
        share(c, 3, left, right, 0, 2)
        share(c, 3, right, left, 2, 2)

    def pass_far(c):
        drain(grads_ref.at[c, 0], g_recv.at[c, 3])
        block = grads_ref.at[c, pl.ds(half * 4, 4), 3]
        remote(block, block, g_send.at[c, 5], g_recv.at[c, 5], (p, first + other)).start()
        drain(grads_ref.at[c, pl.ds(0, 2), pl.ds(0, 3)], g_recv.at[c, 2])
        over_right = lax.rem(right + 4, MEMBERS)
        over_left = lax.rem(left + 4, MEMBERS)
        one, two = (left, right) if c % 2 == 0 else (right, left)
        over_one, over_two = (over_left, over_right) if c % 2 == 0 else (over_right, over_left)
        share(c, 4, one, over_two, 0, 2)
        share(c, 4, two, over_one, 2, 1)

    def rows_out(c):
        drain(grads_ref.at[c, 0, pl.ds(0, 3)], g_recv.at[c, 4])
        drain(grads_ref.at[c, pl.ds(0, 4), 0], g_recv.at[c, 5])

        for h, (back, m) in enumerate(HALVES[c]):
            gate = jnp.concatenate([grads_ref[c, k, GATE[h]] for k in range(MEMBERS)], axis=1)
            up = jnp.concatenate([grads_ref[c, k, UP[h]] for k in range(MEMBERS)], axis=1)
            r = (dot_t(gate, wg_ref[...]) + dot_t(up, wu_ref[...])).astype(BF16)
            r = jnp.concatenate([r[:, LANES * j : LANES * (j + 1)] for j in range(CHUNKS)], axis=0)
            r = dot(unpack_ref[...], r).astype(BF16)
            ret_ref[c, h] = r.reshape(SOURCES, BLOCK, LANES)
            zone = zone_of(back)

            @pl.when(onward[m][0])
            def _():
                def go(i):
                    t = lax.rem(spot + i, SOURCES)
                    remote(
                        ret_ref.at[c, h, t],
                        home_ref.at[m, me],
                        r_send.at[m],
                        r_recv.at[m],
                        (onward[m][1], zone * SOURCES + t),
                    ).start()

                loop(SOURCES, go)

    def selections():
        @pl.when(has_high)
        def _():
            drain(ids_in.at[0], ids_recv.at[0])
            back_ref[0] = selection(ids_in[0, 0:1, 0:TOK]).T.astype(BF16)

        @pl.when(has_low)
        def _():
            drain(ids_in.at[1], ids_recv.at[1])
            back_ref[1] = selection(ids_in[1, 0:1, 0:TOK]).T.astype(BF16)

    def finish(m, wanted):
        @pl.when(wanted)
        def _():
            drain(home_ref.at[m], r_recv.at[m])

            def part(i):
                blocks = [
                    jnp.concatenate([home_ref[m, e * MEMBERS + 2 * i + k] for k in range(2)], axis=1)
                    for e in range(EXPERTS)
                ]
                o = dot(back_ref[m, 0 : CHUNKS * TOK], jnp.concatenate(blocks, axis=0)).astype(BF16)
                for k in range(2):
                    for j in range(CHUNKS):
                        col = pl.multiple_of((2 * i + k) * SLICE + LANES * j, LANES)
                        out_ref[m, :, pl.ds(col, LANES)] = o[
                            TOK * j : TOK * (j + 1), LANES * k : LANES * (k + 1)
                        ]

            loop(4, part)

        @pl.when(jnp.logical_not(wanted))
        def _():
            out_ref[m] = jnp.zeros(out_ref.shape[1:], BF16)

    def build_pack():
        k = lax.rem(iota((1, SOURCES * BLOCK), 1), BLOCK)
        s = iota((1, SOURCES * BLOCK), 1) >> 6
        j = (k * 57) >> 9
        place = jnp.where(k < CHUNKS * CAP, j * GROUP_ROWS + s * CAP + k - j * CAP, -1)

        def part(i):
            at = pl.multiple_of(i * GROUP_ROWS, 16)
            shape = (GROUP_ROWS, SOURCES * BLOCK)
            pack_ref[pl.ds(at, GROUP_ROWS), :] = as_one(iota(shape, 0) + at == place)

        loop(CHUNKS, part)

    def build_unpack():
        r = iota((1, STACK), 1)
        j = jnp.zeros_like(r)
        for i in range(1, CHUNKS):
            j = j + jnp.where(r >= i * GROUP_ROWS, 1, 0)
        r = r - j * GROUP_ROWS
        s = (r * 57) >> 9
        origin = s * BLOCK + j * CAP + r - s * CAP

        def part(i):
            at = pl.multiple_of(i * 128, 128)
            unpack_ref[pl.ds(at, 128), :] = as_one(iota((128, STACK), 0) + at == origin)

        loop(SOURCES * BLOCK // 128, part)

    form(2)
    pl.semaphore_wait(
        barrier, count - 1 + jnp.where(has_low, 1, 0) + jnp.where(has_high, 1, 0)
    )
    dispatch(1)
    form(0)
    dispatch(0)
    form(1)
    form(3)
    dispatch(2)
    dispatch(3)

    to_low = remote(ids_out.at[0], ids_in.at[0], ids_send.at[0], ids_recv.at[0], (low, me))
    to_high = remote(ids_out.at[1], ids_in.at[1], ids_send.at[1], ids_recv.at[1], (high, me))

    @pl.when(has_low)
    def _():
        to_low.start()

    @pl.when(has_high)
    def _():
        to_high.start()

    build_pack()
    weights[0].wait()
    weights[3].wait()
    weights[4].wait()
    hidden(0)
    reduce_x(0)
    activation(0)
    hidden(1)
    pass_on(0)
    hidden(2)
    reduce_x(1)
    pass_far(0)
    activation(1)
    build_unpack()
    hidden(3)
    reduce_x(2)
    pass_on(1)
    activation(2)
    pass_far(1)
    weights[1].wait()
    weights[2].wait()
    reduce_x(3)
    pass_on(2)
    rows_out(1)
    activation(3)
    pass_far(2)
    pass_on(3)
    selections()
    rows_out(2)
    pass_far(3)
    rows_out(0)
    rows_out(3)
    finish(0, has_high)
    finish(1, has_low)

    @pl.when(has_low)
    def _():
        drain(ids_in.at[0], ids_send.at[0])
        drain(home_ref.at[0], r_send.at[0])

    @pl.when(has_high)
    def _():
        drain(ids_in.at[1], ids_send.at[1])
        drain(home_ref.at[1], r_send.at[1])

    for c in range(ZONES):
        drain(recv_ref.at[c, pl.ds(0, SOURCES - (1 if c == 0 else 0))], d_send.at[c])
        drain(xin_ref.at[c], x_send.at[c])
        drain(yin_ref.at[c], s_send.at[c])
        drain(grads_ref.at[c, 0, pl.ds(0, 3)], g_send.at[c, 0])
        drain(grads_ref.at[c, pl.ds(0, 2)], g_send.at[c, 1])
        drain(grads_ref.at[c, pl.ds(0, 2), pl.ds(0, 3)], g_send.at[c, 2])
        drain(grads_ref.at[c, 0], g_send.at[c, 3])
        drain(grads_ref.at[c, 0, pl.ds(0, 3)], g_send.at[c, 4])
        drain(grads_ref.at[c, pl.ds(0, 4), 0], g_send.at[c, 5])


def body(out_grad, expert_ids, gate_weights, valid, gate_pre, up_pre, w_gate, w_up, w_down):
    count = lax.axis_size("expert")
    ids = expert_ids.reshape(2, 1, TOK)
    weight = gate_weights.reshape(2, 1, TOK)
    vmem = pl.BlockSpec(memory_space=pltpu.VMEM)
    hbm = pl.BlockSpec(memory_space=pl.ANY)
    dma = pltpu.SemaphoreType.DMA
    out = pl.pallas_call(
        kernel,
        out_shape=jax.ShapeDtypeStruct(out_grad.shape[1:], BF16),
        in_specs=[vmem] * 3 + [hbm] * 6,
        out_specs=vmem,
        scratch_shapes=[
            pltpu.VMEM(out_grad.shape[1:], BF16),
            pltpu.VMEM(gate_pre.shape[1:], BF16),
            pltpu.VMEM(up_pre.shape[1:], BF16),
            pltpu.VMEM(w_gate.shape[1:], BF16),
            pltpu.VMEM(w_up.shape[1:], BF16),
            pltpu.VMEM(w_down.shape[1:], BF16),
            pltpu.VMEM((2, EXPERTS * BLOCK, 8 * TOK), BF16),
            pltpu.VMEM((2, 8 * TOK, EXPERTS * BLOCK), BF16),
            pltpu.VMEM((2, EXPERTS, LANES), jnp.int32),
            pltpu.VMEM((2, EXPERTS, LANES), jnp.int32),
            pltpu.VMEM((STACK, SOURCES * BLOCK), BF16),
            pltpu.VMEM((SOURCES * BLOCK, STACK), BF16),
            pltpu.VMEM((2, EXPERTS * BLOCK, 1), F32),
            pltpu.VMEM((count, 2, BLOCK, LANES), BF16),
            pltpu.VMEM((ZONES, SOURCES, 2, BLOCK, LANES), BF16),
            pltpu.VMEM((2 * GROUP_ROWS, SLICE), BF16),
            pltpu.VMEM((ZONES, 4, 2 * GROUP_ROWS, LANES), BF16),
            pltpu.VMEM((ZONES, 4, 2 * GROUP_ROWS, LANES), BF16),
            pltpu.VMEM((ZONES, 4, 2 * GROUP_ROWS, LANES), F32),
            pltpu.VMEM((ZONES, 4, 2 * GROUP_ROWS, LANES), BF16),
            pltpu.VMEM((ZONES, 3, 2 * GROUP_ROWS, LANES), BF16),
            pltpu.VMEM((ZONES, MEMBERS, 4, GROUP_ROWS, LANES), BF16),
            pltpu.VMEM((ZONES, 2, SOURCES, BLOCK, LANES), BF16),
            pltpu.VMEM((2, count, BLOCK, LANES), BF16),
            dma((6,)),
            dma((2,)),
            dma((2,)),
            dma((ZONES,)),
            dma((ZONES,)),
            dma,
            dma((ZONES,)),
            dma((ZONES,)),
            dma((ZONES,)),
            dma((ZONES,)),
            dma((ZONES, 6)),
            dma((ZONES, 6)),
            dma((2,)),
            dma((2,)),
        ],
        compiler_params=pltpu.CompilerParams(
            collective_id=0, has_side_effects=True, vmem_limit_bytes=58 * 2**20
        ),
    )(ids, weight, valid[0], out_grad[0], gate_pre[0], up_pre[0], w_gate[0], w_up[0], w_down[0])
    return out[None]


def solution(mesh):
    placed = (
        P("pipe", None, "expert", None),
        P("pipe", None, "expert", None),
        P("pipe", None, "expert", None),
        P("pipe", None, "expert"),
        P("pipe", None, None, "expert"),
        P("pipe", None, None, "expert"),
        P("pipe", "expert", None),
        P("pipe", "expert", None),
        P("pipe", None, "expert"),
    )
    return jax.shard_map(
        body, mesh=mesh, in_specs=placed, out_specs=P("pipe", None, "expert", None), check_vma=False
    )
```
